32 devices in a mesh: period: 4 (over x, core), bus: 8 (over z, y).
Axes of the slice: x: 2, y: 2, z: 4, core: 2. Of those that a mesh axis runs over, the one named last changes fastest.
Arguments:
- gain: bfloat16 [4, 2048, 2048], P('period', 'bus'), may hold values from -0.15 to 1.15
- schur: bfloat16 [4, 2048, 2048], P('period', 'bus'), may hold values from -0.0625 to 0.0625
- inverse_blocks: bfloat16 [4, 10240, 1280], P('period', 'bus'), may hold values from -0.15625 to 0.15625
- sensitivity: bfloat16 [10240, 2048], P('bus'), may hold values from -0.078125 to 0.078125
- residual_bus: float32 [4, 10240, 512], P('period', 'bus'), may hold values from -6 to 6
- unit_rhs: float32 [4, 2048, 512], P('period', 'bus'), may hold values from -6 to 6
- start_state: float32 [2048, 512], P('bus'), may hold values from -6 to 6
- active_set: int32 [4, 10240], P('period', 'bus'), may hold values 0 or 1
- unit_bus: int32 [2048], replicated, may hold values from 0 to 10239
Outputs:
- storage_path: float32 [4, 2048, 512], P('period', 'bus')
- costate: float32 [4, 2048, 512], P('period', 'bus')
- bus_update: float32 [4, 10240, 512], P('period', 'bus')
The draws below stay inside these ranges and needn't reach their ends.
All inputs are finite; a program needn't handle non-finite values. No bound on the sum of `active_set` on one device may be relied on, other than what follows from the above.
Results may differ from the reference program's by a relative error of at most 0.008.
Values may be sent and summed in bfloat16 or wider, within the bound.
No kernel may reach another device: no remote copies, remote signals or barrier semaphores. Data moves between devices by JAX's collectives and lax.ppermute only.
A program may use at most 64 MiB of HBM per device.

```python
import math
import jax
import jax.numpy as jnp
from jax import lax

K = 2048
NB = 10240
R = 512
TIME_PERIODS = 4
BUS_DEV = 1280
N_BUS = 8


def draw_gain(key, part):
    random_keys = jax.random.split(jax.random.fold_in(key, 17), 5)
    low_rate, high_rate = (0.02, 2.0)
    ramp_limit = jnp.exp(jax.random.uniform(random_keys[0], (1, K), jnp.float32, math.log(low_rate), math.log(high_rate)))
    regularizer_shift = 2.0 ** jax.random.uniform(random_keys[1], (TIME_PERIODS, 1), jnp.float32, -0.5, 0.5)
    surge_amount = jax.random.uniform(random_keys[2], (TIME_PERIODS, 1), jnp.float32) < 0.2
    cholesky_factor = jax.random.uniform(random_keys[3], (TIME_PERIODS, 1), jnp.float32, 0.5, 0.8)
    diagonal_entries = jnp.exp(-ramp_limit * regularizer_shift) * jnp.where(surge_amount, cholesky_factor, 1.0)
    spread = jnp.clip(jax.random.normal(random_keys[4], (TIME_PERIODS, K, K), jnp.float32), -4.0, 4.0) * (0.25 / math.sqrt(K))
    return (spread + jnp.eye(K, dtype=jnp.float32)[None] * diagonal_entries[:, :, None]).astype(jnp.bfloat16)


def place_ends(values, key, low, high):
    extent = values.shape
    index_at = [jax.random.randint(jax.random.fold_in(key, axis), (), 0, extent[axis]) for axis in range(len(extent))]
    values = values.at[tuple(index_at)].set(low)
    longest = extent.index(max(extent))
    index_at[longest] = (index_at[longest] + 1) % extent[longest]
    return values.at[tuple(index_at)].set(high)


def spiked(result, key, source, target, blocks, factor):
    def block_of(position):
        return (jnp.arange(result.shape[position]) // (result.shape[position] // blocks)).reshape((-1,) + (1,) * (result.ndim - 1 - position))

    near = jax.random.permutation(key, blocks)[block_of(target)]
    other_side = (block_of(target) + blocks // 2) % blocks
    return jnp.where((block_of(source) == near) | (block_of(source) == other_side), factor * result, result)


def levels(key, shape, pieces, least, largest):
    level, own = 1.0, jax.random.fold_in(key, 6)
    for dim, parts in pieces:
        heights = jnp.exp(jax.random.uniform(jax.random.fold_in(own, dim), (parts,), jnp.float32, least / len(pieces), largest / len(pieces)))
        level = level * jnp.repeat(heights, shape[dim] // parts).reshape([-1 if axis == dim else 1 for axis in range(len(shape))])
    return level


def noise(own_key, dims, scale, limit, shards=(), held_as=jnp.bfloat16):
    array = jax.random.normal(own_key, dims, jnp.float32) * scale
    if len(shards) > 0:
        array = levels(own_key, dims, shards, -0.22, 0.18) * array
    return jnp.clip(array, min=-limit, max=limit).astype(held_as)


def gaussian_with(key, dims, deviation, reach, shards, heavy, held_as=jnp.bfloat16):
    result = deviation * jax.random.normal(key, dims, jnp.float32)
    if shards:
        result = result * levels(key, dims, shards, -0.22, 0.18)
    return jnp.clip(spiked(result, jax.random.fold_in(key, 3), *heavy), -reach, reach).astype(held_as)


def setup_inputs(seed: int = 0) -> dict:
    streams_of = jax.random.split(jax.random.key(seed), 10)
    gain = draw_gain(jax.random.fold_in(streams_of[9], 71), 0)
    schur = noise(streams_of[1], (TIME_PERIODS, K, K), (4 * K) ** -0.5, 0.0625, ((0, 4), (1, 8)))
    inverse_blocks = noise(streams_of[2], (TIME_PERIODS, NB, BUS_DEV), (NB // N_BUS) ** -0.5, 0.15625, ((0, 4), (1, 8)))
    sensitivity = gaussian_with(streams_of[3], (NB, K), NB ** -0.5, 0.078125, ((0, 8),), (0, 1, 8, 2.0))
    residual_bus = noise(streams_of[4], (TIME_PERIODS, NB, R), 1.0, 6.0, ((0, 4), (1, 8)), jnp.float32)
    unit_rhs = noise(streams_of[5], (TIME_PERIODS, K, R), 1.0, 6.0, ((0, 4), (1, 8)), jnp.float32)
    start_state = noise(streams_of[6], (K, R), 1.0, 6.0, ((0, 8),), jnp.float32)
    active_set = place_ends((jax.random.randint(streams_of[7], (TIME_PERIODS, NB), 0, 4) < 1).astype(jnp.int32), jax.random.fold_in(streams_of[7], 1), 0, 1)
    unit_bus = place_ends(jax.random.randint(streams_of[8], (K,), 0, NB), jax.random.fold_in(streams_of[8], 1), 0, NB - 1).astype(jnp.int32)
    return {"gain": gain, "schur": schur, "inverse_blocks": inverse_blocks, "sensitivity": sensitivity, "residual_bus": residual_bus, "unit_rhs": unit_rhs, "start_state": start_state, "active_set": active_set, "unit_bus": unit_bus}


def partition_apply(blocks, values):
    rows = NB // N_BUS
    rounded = lax.optimization_barrier(values)
    grouped = rounded.astype(jnp.float32).reshape(N_BUS, rows, R)
    matrix = blocks.astype(jnp.float32).reshape(N_BUS, rows, rows)
    return jnp.einsum('qij,qjr->qir', matrix, grouped).reshape(NB, R)


def reference(gain, schur, inverse_blocks, sensitivity, residual_bus, unit_rhs, start_state, active_set, unit_bus):
    weighted = residual_bus * (1.0 + 3.0 * active_set[:, :, None].astype(jnp.float32))
    net_in = weighted.astype(jnp.bfloat16)
    unit_right = []
    for period in range(TIME_PERIODS):
        bus_solve = partition_apply(inverse_blocks[period], net_in[period]).astype(jnp.bfloat16)
        unit_right.append(unit_rhs[period] + jnp.dot(sensitivity.T, bus_solve, preferred_element_type=jnp.float32))
    later = jnp.zeros((K, R), jnp.float32)
    costates = [None] * TIME_PERIODS
    for period in reversed(range(TIME_PERIODS)):
        later = unit_right[period] + jnp.dot(gain[period].T, later.astype(jnp.bfloat16), preferred_element_type=jnp.float32)
        costates[period] = later
    current = start_state
    states = []
    updates = []
    for period in range(TIME_PERIODS):
        state_round = current.astype(jnp.bfloat16)
        costate_round = costates[period].astype(jnp.bfloat16)
        injection = jax.ops.segment_sum(state_round.astype(jnp.float32), unit_bus, num_segments=NB)
        network = (weighted[period] - injection).astype(jnp.bfloat16)
        updates.append(partition_apply(inverse_blocks[period], network))
        current = jnp.dot(gain[period], state_round, preferred_element_type=jnp.float32) - jnp.dot(schur[period], costate_round, preferred_element_type=jnp.float32)
        states.append(current)
    return jnp.stack(states), jnp.stack(costates), jnp.stack(updates)
```

```python
import jax
import jax.numpy as jnp
from jax import lax
from jax.sharding import PartitionSpec as P

BOTH = ("period", "bus")
F32 = jnp.float32
BF16 = jnp.bfloat16


def bus_send(block, flip, periods):
    size = lax.axis_size("bus")
    route = [(p * size + b, p * size + (b ^ flip)) for p in periods for b in range(size)]
    return lax.ppermute(block, BOTH, route)


def period_send(block, source, target):
    size = lax.axis_size("bus")
    route = [(source * size + b, target * size + b) for b in range(size)]
    return lax.ppermute(block, BOTH, route)


def in_planes():
    return lax.axis_size("bus") == 8


def gather_parts(block, periods):
    parts = {0: block}
    for flip in (6, 4, 2):
        parts[flip] = bus_send(block, flip, periods)
    for flip in (0, 2, 4, 6):
        parts[flip ^ 1] = bus_send(parts[flip], 1, periods)
    return parts


def gather_rows(block, periods):
    if not in_planes():
        return lax.all_gather(block, "bus", axis=0, tiled=True)
    rank = lax.axis_index("bus")
    rows = block.shape[0]
    parts = gather_parts(block, periods)
    whole = jnp.zeros((8 * rows, block.shape[1]), block.dtype)
    for flip, part in parts.items():
        whole = lax.dynamic_update_slice(whole, part, ((rank ^ flip) * rows, 0))
    return whole


def reduce_rows(partial, periods):
    if not in_planes():
        return lax.psum_scatter(
            partial.astype(BF16), "bus", scatter_dimension=0, tiled=True
        ).astype(F32)
    rank = lax.axis_index("bus")
    rows = partial.shape[0] // 8

    def chunk(owner):
        return lax.dynamic_slice_in_dim(partial, owner * rows, rows, 0)

    total = None
    for flip in (6, 4, 2, 0):
        there = bus_send(chunk(rank ^ 1 ^ flip).astype(BF16), 1, periods)
        here = chunk(rank ^ flip) + there.astype(F32)
        if flip:
            here = bus_send(here.astype(BF16), flip, periods).astype(F32)
        total = here if total is None else total + here
    return total


def rows_to_columns(block, periods):
    size = lax.axis_size("bus")
    rows = block.shape[0] // size
    units = block.shape[1]
    if not in_planes():
        swapped = lax.all_to_all(block.reshape(size, rows, units), "bus", 0, 0)
        return jnp.transpose(swapped, (1, 0, 2)).reshape(rows, size * units)
    rank = lax.axis_index("bus")

    def chunk(owner):
        return lax.dynamic_slice_in_dim(block, owner * rows, rows, 0)

    flips = (0, 2, 4, 6)
    there = bus_send(jnp.stack([chunk(rank ^ 1 ^ flip) for flip in flips]), 1, periods)
    whole = jnp.zeros((size, rows, units), block.dtype)
    for place, flip in enumerate(flips):
        pair = jnp.stack([chunk(rank ^ flip), there[place]])
        if flip:
            pair = bus_send(pair, flip, periods)
        whole = lax.dynamic_update_slice(whole, pair[:1], (rank ^ flip, 0, 0))
        whole = lax.dynamic_update_slice(whole, pair[1:], (rank ^ flip ^ 1, 0, 0))
    return jnp.transpose(whole, (1, 0, 2)).reshape(rows, size * units)


def times(left, right):
    return jnp.dot(left, right, preferred_element_type=F32)


def times_t(left, right):
    return lax.dot_general(left, right, (((1,), (1,)), ((), ())), preferred_element_type=F32)


def body(
    gain,
    schur,
    inverse_blocks,
    sensitivity,
    residual_bus,
    unit_rhs,
    start_state,
    active_set,
    unit_bus,
):
    gain, schur, inverse = gain[0], schur[0], inverse_blocks[0]
    unit_rows = gain.shape[0]
    bus_rows = inverse.shape[0]
    period = lax.axis_index("period")
    rank = lax.axis_index("bus")
    groups = lax.axis_size("period")
    last = groups - 1
    everyone = tuple(range(groups))
    inner = tuple(range(1, last))
    outer = (0, last)

    weighted = residual_bus[0] * (1.0 + 3.0 * active_set[0][:, None].astype(F32))
    solve = times(inverse, weighted.astype(BF16)).astype(BF16)
    partial = lax.dot_general(
        solve, sensitivity, (((0,), (0,)), ((), ())), preferred_element_type=F32
    )
    own_rhs = unit_rhs[0].T
    own_place = (0, rank * unit_rows)
    own_part = lax.dynamic_slice(partial, own_place, own_rhs.shape)
    partial = lax.dynamic_update_slice(partial, own_part + own_rhs, own_place)

    gain_inner = gather_rows(gain, inner)
    unit_right = reduce_rows(partial, everyone)
    first_schur = period_send(schur, 0, last)
    outer_block = jnp.where(period == last, first_schur, gain)
    outer_block, unit_right = lax.optimization_barrier((outer_block, unit_right))
    matrix_outer = gather_rows(outer_block, outer)
    start = rows_to_columns(start_state.T.astype(BF16), everyone)

    costate = unit_right.astype(BF16)
    for target in range(last - 1, -1, -1):
        later = period_send(costate, target + 1, target)
        matrix = matrix_outer if target == 0 else gain_inner
        current = (unit_right + times(later, matrix)).astype(BF16)
        costate = jnp.where(period == target, current, costate)

    at_last = period_send(costate, 0, last)
    coupled = period_send(times_t(at_last, matrix_outer).astype(BF16), last, 0)
    costate_all = gather_rows(costate, everyone)
    coupling = times_t(costate_all, schur)
    coupling_cols = rows_to_columns(coupling.astype(BF16), everyone).astype(F32)

    state = start
    advanced = times_t(start, matrix_outer) - coupled.astype(F32)
    for target in range(1, groups):
        arrived = period_send(advanced.astype(BF16), target - 1, target)
        state = jnp.where(period == target, arrived, state)
        if target < last:
            advanced = times_t(arrived, gain_inner) - coupling_cols

    state_all = gather_rows(state, everyone)
    storage = times_t(gain, state_all) - coupling.T
    own_costate = lax.dynamic_slice_in_dim(costate_all, rank * unit_rows, unit_rows, 1)
    bus_ids = rank * bus_rows + jnp.arange(bus_rows, dtype=jnp.int32)
    placement = (unit_bus[None, :] == bus_ids[:, None]).astype(BF16)
    injection = times_t(placement, state_all)
    update = times(inverse, (weighted - injection).astype(BF16))
    return (storage[None], own_costate.T.astype(F32)[None], update[None])


def solution(mesh):
    by_period = P("period", "bus", None)
    placed = (
        by_period,
        by_period,
        by_period,
        P("bus", None),
        by_period,
        by_period,
        P("bus", None),
        P("period", "bus"),
        P(),
    )
    return jax.shard_map(
        body,
        mesh=mesh,
        in_specs=placed,
        out_specs=(by_period, by_period, by_period),
        check_vma=False,
    )
```

```python
import functools

import jax
import jax.numpy as jnp
from jax import lax
from jax.experimental import pallas as pl
from jax.experimental.pallas import tpu as pltpu
from jax.sharding import PartitionSpec as P

BOTH = ("period", "bus")
F32 = jnp.float32
BF16 = jnp.bfloat16
EVEN = (0, 2, 4, 6)
MIB = 1 << 20


def bus_send(block, flip, periods):
    size = lax.axis_size("bus")
    route = [(p * size + b, p * size + (b ^ flip)) for p in periods for b in range(size)]
    return lax.ppermute(block, BOTH, route)


def period_send(block, source, target):
    size = lax.axis_size("bus")
    route = [(source * size + b, target * size + b) for b in range(size)]
    return lax.ppermute(block, BOTH, route)


def times(left, right):
    return jnp.dot(left, right, preferred_element_type=F32)


def times_t(left, right):
    return lax.dot_general(left, right, (((1,), (1,)), ((), ())), preferred_element_type=F32)


def gather_parts(block, periods):
    parts = {0: block}
    for flip in (6, 4, 2):
        parts[flip] = bus_send(block, flip, periods)
    for flip in EVEN:
        parts[flip ^ 1] = bus_send(parts[flip], 1, periods)
    return [parts[flip] for flip in range(8)]


def reduce_parts(parts, periods):
    total = None
    for flip in (6, 4, 2, 0):
        here = parts[flip] + bus_send(parts[flip ^ 1], 1, periods).astype(F32)
        if flip:
            here = bus_send(here.astype(BF16), flip, periods).astype(F32)
        total = here if total is None else total + here
    return total


def swap_parts(keep, send, periods):
    there = bus_send(send, 1, periods)
    parts = {}
    for place, flip in enumerate(EVEN):
        pair = jnp.stack([keep[place], there[place]])
        if flip:
            pair = bus_send(pair, flip, periods)
        parts[flip], parts[flip ^ 1] = pair[0], pair[1]
    return [parts[flip] for flip in range(8)]


def in_vmem():
    return pl.BlockSpec(memory_space=pltpu.VMEM)


def anywhere():
    return pl.BlockSpec(memory_space=pl.ANY)


def in_smem():
    return pl.BlockSpec(memory_space=pltpu.SMEM)


def kernel_call(kernel, out_shape, in_specs, scratch, flops, bytes_accessed):
    return pl.pallas_call(
        kernel,
        out_shape=out_shape,
        in_specs=in_specs,
        out_specs=jax.tree.map(lambda _: in_vmem(), out_shape),
        scratch_shapes=scratch,
        compiler_params=pltpu.CompilerParams(vmem_limit_bytes=48 * MIB),
        cost_estimate=pl.CostEstimate(
            flops=flops, bytes_accessed=bytes_accessed, transcendentals=0
        ),
    )


def front_kernel(
    rank_ref, active, rhs, residual_hbm, inverse_hbm, sens_hbm,
    k0, s0, k1, s1, k2, s2, k3, s3,
    residual, inverse, sens, net, solve_t, partial, sems,
):
    rank = rank_ref[0]
    loads = [
        pltpu.make_async_copy(residual_hbm, residual, sems.at[0]),
        pltpu.make_async_copy(inverse_hbm, inverse, sems.at[1]),
        pltpu.make_async_copy(sens_hbm, sens, sems.at[2]),
    ]
    for load in loads:
        load.start()
    loads[0].wait()
    net[...] = (residual[...] * (1.0 + 3.0 * active[...].astype(F32))).astype(BF16)
    loads[1].wait()
    blocks = inverse.shape[0] // 256

    @pl.loop(0, blocks)
    def _(i):
        rows = pl.ds(pl.multiple_of(i * 256, 256), 256)
        solve_t[:, rows] = times(inverse[rows, :], net[...]).T.astype(BF16)

    loads[2].wait()

    @pl.loop(0, sens.shape[1] // 256)
    def _(i):
        columns = pl.ds(pl.multiple_of(i * 256, 256), 256)
        partial[:, columns] = times(solve_t[...], sens[:, columns])

    units = rhs.shape[0]
    own = pl.ds(pl.multiple_of(rank * units, units), units)
    partial[:, own] += rhs[...].T
    rows = k0.shape[0]
    for flip, out in enumerate((k0, s0, k1, s1, k2, s2, k3, s3)):
        owner = pl.multiple_of((rank ^ flip) * rows, rows)
        out[...] = partial[pl.ds(owner, rows), :].astype(out.dtype)


def front(rank, active, rhs, residual, inverse, sens):
    buses, columns = residual.shape
    units = sens.shape[1]
    rows = columns // 8
    keep = jax.ShapeDtypeStruct((rows, units), F32)
    send = jax.ShapeDtypeStruct((rows, units), BF16)
    return kernel_call(
        front_kernel,
        [keep, send] * 4,
        [in_smem(), in_vmem(), in_vmem(), anywhere(), anywhere(), anywhere()],
        [
            pltpu.VMEM((buses, columns), F32),
            pltpu.VMEM((buses, buses), BF16),
            pltpu.VMEM((buses, units), BF16),
            pltpu.VMEM((buses, columns), BF16),
            pltpu.VMEM((columns, buses), BF16),
            pltpu.VMEM((columns, units), F32),
            pltpu.SemaphoreType.DMA((3,)),
        ],
        2 * buses * columns * (buses + units),
        24 * MIB,
    )(rank, active, rhs, residual, inverse, sens)


def weight_loads(rank, weights, held, sems):
    units = held.shape[1]
    loads = []
    for flip in range(8):
        owner = pl.multiple_of((rank ^ flip) * units, units)
        source = weights.at[pl.ds(owner, units)]
        loads.append(pltpu.make_async_copy(source, held.at[flip], sems.at[flip]))
    return loads


def backward_kernel(rank_ref, vector, base, *refs):
    weights, out, held, total, sems = refs
    rank = rank_ref[0]
    loads = weight_loads(rank, weights, held, sems)
    for load in loads:
        load.start()
    units = held.shape[1]
    total[...] = base[...]
    for flip, load in enumerate(loads):
        load.wait()
        own = pl.ds(pl.multiple_of((rank ^ flip) * units, units), units)
        total[...] += times(vector[:, own], held[flip])
    out[...] = total[...].astype(out.dtype)


def forward_kernel(subtract, rank_ref, vector, *refs):
    weights, refs = refs[0], refs[1:]
    terms, (out, held, sems) = (refs[:8], refs[8:]) if subtract else (None, refs)
    rank = rank_ref[0]
    loads = weight_loads(rank, weights, held, sems)
    for load in loads:
        load.start()
    units = held.shape[1]
    for flip, load in enumerate(loads):
        load.wait()
        own = pl.ds(pl.multiple_of((rank ^ flip) * units, units), units)
        product = times_t(vector[...], held[flip])
        if subtract:
            product = product - terms[flip][...].astype(F32)
        out[:, own] = product.astype(out.dtype)


def backward(rank, vector, base, weights):
    rows, whole = vector.shape
    units = weights.shape[0] // 8
    return kernel_call(
        backward_kernel,
        jax.ShapeDtypeStruct((rows, whole), BF16),
        [in_smem(), in_vmem(), in_vmem()] + [anywhere()],
        [
            pltpu.VMEM((8, units, whole), BF16),
            pltpu.VMEM((rows, whole), F32),
            pltpu.SemaphoreType.DMA((8,)),
        ],
        2 * rows * whole * whole,
        2 * whole * whole,
    )(rank, vector, base, weights)


def forward(rank, vector, weights, terms=()):
    rows, whole = vector.shape
    units = weights.shape[0] // 8
    return kernel_call(
        functools.partial(forward_kernel, bool(terms)),
        jax.ShapeDtypeStruct((rows, whole), BF16),
        [in_smem(), in_vmem()] + [anywhere()] + [in_vmem()] * len(terms),
        [pltpu.VMEM((8, units, whole), BF16), pltpu.SemaphoreType.DMA((8,))],
        2 * rows * whole * whole,
        2 * whole * whole,
    )(rank, vector, weights, *terms)


def assemble(rank, first, second, whole):
    rows = first[0].shape[0]
    for flip in range(8):
        owner = pl.multiple_of((rank ^ flip) * rows, rows)
        block = first[flip][...]
        if flip and second:
            block = block + second[flip - 1][...]
        whole[pl.ds(owner, rows), :] = block


def couple_kernel(rank_ref, schur, *refs):
    parts, (keep, send, product, whole) = refs[:8], refs[8:]
    rank = rank_ref[0]
    assemble(rank, parts, (), whole)
    product[...] = times_t(whole[...], schur[...])
    rows = keep.shape[1]
    for place, flip in enumerate(EVEN):
        keep[place] = product[pl.ds(pl.multiple_of((rank ^ flip) * rows, rows), rows), :].astype(BF16)
        send[place] = product[pl.ds(pl.multiple_of((rank ^ flip ^ 1) * rows, rows), rows), :].astype(BF16)


def couple(rank, schur, parts):
    units, whole = schur.shape
    rows = parts[0].shape[0]
    piece = jax.ShapeDtypeStruct((4, rows, units), BF16)
    return kernel_call(
        couple_kernel,
        [piece, piece],
        [in_smem(), in_vmem()] + [in_vmem()] * 8,
        [pltpu.VMEM((8 * rows, units), F32), pltpu.VMEM((8 * rows, whole), BF16)],
        16 * rows * whole * units,
        4 * MIB,
    )(rank, schur, *parts)


def costate_kernel(rank_ref, schur, *refs):
    first, second, (costate, coupling, whole) = refs[:8], refs[8:15], refs[15:]
    rank = rank_ref[0]
    assemble(rank, first, second, whole)
    coupling[...] = times_t(schur[...], whole[...])
    units = schur.shape[0]
    own = pl.ds(pl.multiple_of(rank * units, units), units)
    costate[...] = whole[:, own].astype(F32).T


def costate_out(rank, schur, first, second):
    units, whole = schur.shape
    rows = first[0].shape[0]
    out = jax.ShapeDtypeStruct((units, 8 * rows), F32)
    return kernel_call(
        costate_kernel,
        [out, out],
        [in_smem(), in_vmem()] + [in_vmem()] * 15,
        [pltpu.VMEM((8 * rows, whole), BF16)],
        16 * rows * whole * units,
        6 * MIB,
    )(rank, schur, *first, *second[1:])


def final_kernel(rank_ref, unit_bus, active, coupling, gain, residual_hbm, inverse_hbm, *refs):
    first, second = refs[:8], refs[8:15]
    storage, update, residual, inverse, whole, network, sems = refs[15:]
    rank = rank_ref[0]
    loads = [
        pltpu.make_async_copy(residual_hbm, residual, sems.at[0]),
        pltpu.make_async_copy(inverse_hbm, inverse, sems.at[1]),
    ]
    for load in loads:
        load.start()
    assemble(rank, first, second, whole)
    loads[0].wait()
    buses = inverse.shape[0]

    @pl.loop(0, buses // 256)
    def _(i):
        rows = pl.ds(pl.multiple_of(i * 256, 256), 256)
        ids = rank * buses + i * 256 + lax.broadcasted_iota(jnp.int32, (256, 1), 0)
        placed = (unit_bus[...] == ids).astype(BF16)
        injection = times_t(placed, whole[...])
        weighted = residual[rows, :] * (1.0 + 3.0 * active[rows, :].astype(F32))
        network[rows, :] = (weighted - injection).astype(BF16)

    storage[...] = times_t(gain[...], whole[...]) - coupling[...]
    loads[1].wait()

    @pl.loop(0, buses // 256)
    def _(i):
        rows = pl.ds(pl.multiple_of(i * 256, 256), 256)
        update[rows, :] = times(inverse[rows, :], network[...])


def final(rank, unit_bus, active, coupling, gain, residual, inverse, first, second):
    buses, columns = residual.shape
    units, whole = gain.shape
    return kernel_call(
        final_kernel,
        [
            jax.ShapeDtypeStruct((units, columns), F32),
            jax.ShapeDtypeStruct((buses, columns), F32),
        ],
        [in_smem()] + [in_vmem()] * 4 + [anywhere()] * 2 + [in_vmem()] * 15,
        [
            pltpu.VMEM((buses, columns), F32),
            pltpu.VMEM((buses, buses), BF16),
            pltpu.VMEM((columns, whole), BF16),
            pltpu.VMEM((buses, columns), BF16),
            pltpu.SemaphoreType.DMA((2,)),
        ],
        2 * columns * (buses * buses + (buses + units) * whole),
        24 * MIB,
    )(rank, unit_bus, active, coupling, gain, residual, inverse, *first, *second[1:])


def plane_body(
    gain, schur, inverse, sens, residual, unit_rhs, start_state, active, unit_bus
):
    period = lax.axis_index("period")
    rank = lax.axis_index("bus").reshape(1)
    last = lax.axis_size("period") - 1
    everyone = tuple(range(last + 1))
    inner = tuple(range(1, last))
    outer = (0, last)
    rows = residual.shape[1] // 8

    first_schur = period_send(schur, 0, last)
    outer_block = jnp.where(period == last, first_schur, gain)
    gain_inner = matrix_outer = lax.all_gather(outer_block, "bus", axis=0, tiled=True)
    terms = front(rank, active, unit_rhs, residual, inverse, sens)
    unit_right = reduce_parts(terms, everyone)

    start_t = start_state.T.astype(BF16)

    def start_piece(owner):
        return lax.dynamic_slice_in_dim(start_t, owner * rows, rows, 0)

    keep = jnp.stack([start_piece(rank[0] ^ flip) for flip in EVEN])
    send = jnp.stack([start_piece(rank[0] ^ flip ^ 1) for flip in EVEN])
    pieces = jnp.stack(swap_parts(keep, send, everyone))
    ordered = jnp.take(pieces, jnp.arange(8, dtype=jnp.int32) ^ rank[0], axis=0)
    start = jnp.transpose(ordered, (1, 0, 2)).reshape(rows, -1)

    costate = unit_right.astype(BF16)
    for target in range(last - 1, 0, -1):
        later = period_send(costate, target + 1, target)
        costate = jnp.where(period == target, backward(rank, later, unit_right, gain_inner), costate)
    inner_costates = gather_parts(costate, inner)
    keep, send = couple(rank, schur, inner_costates)
    coupled_inner = swap_parts(keep, send, inner)
    later = period_send(costate, 1, 0)
    costate = jnp.where(period == 0, backward(rank, later, unit_right, matrix_outer), costate)

    at_last = period_send(costate, 0, last)
    coupled = period_send(forward(rank, at_last, matrix_outer), last, 0)
    outer_costates = gather_parts(costate, outer)
    costate_rows, coupling = costate_out(rank, schur, outer_costates, inner_costates)

    state = start
    driven = forward(rank, start, matrix_outer)
    advanced = (driven.astype(F32) - coupled.astype(F32)).astype(BF16)
    for target in range(1, last + 1):
        arrived = period_send(advanced, target - 1, target)
        state = jnp.where(period == target, arrived, state)
        if target == last - 1:
            early_states = gather_parts(state, everyone[:-1])
        if target < last:
            advanced = forward(rank, arrived, gain_inner, coupled_inner)
    last_states = gather_parts(state, (last,))
    storage, update = final(
        rank, unit_bus, active, coupling, gain, residual, inverse, last_states, early_states
    )
    return storage, costate_rows, update


def plain_body(
    gain, schur, inverse, sens, residual, unit_rhs, start_state, active, unit_bus
):
    period = lax.axis_index("period")
    rank = lax.axis_index("bus")
    size = lax.axis_size("bus")
    groups = lax.axis_size("period")
    units, whole = gain.shape
    buses, columns = residual.shape
    rows = columns // size

    def gathered(block):
        return lax.all_gather(block, "bus", axis=0, tiled=True)

    def to_columns(block):
        swapped = lax.all_to_all(block.reshape(size, rows, units), "bus", 0, 0)
        return jnp.transpose(swapped, (1, 0, 2)).reshape(rows, whole)

    weighted = residual * (1.0 + 3.0 * active.astype(F32))
    solve = times(inverse, weighted.astype(BF16)).astype(BF16)
    partial = lax.dot_general(solve, sens, (((0,), (0,)), ((), ())), preferred_element_type=F32)
    place = (0, rank * units)
    own = lax.dynamic_slice(partial, place, (columns, units)) + unit_rhs.T
    partial = lax.dynamic_update_slice(partial, own, place).astype(BF16)
    unit_right = lax.psum_scatter(partial, "bus", scatter_dimension=0, tiled=True).astype(F32)
    gain_whole = gathered(gain)
    costate = unit_right.astype(BF16)
    for target in range(groups - 2, -1, -1):
        later = period_send(costate, target + 1, target)
        current = (unit_right + times(later, gain_whole)).astype(BF16)
        costate = jnp.where(period == target, current, costate)
    costate_whole = gathered(costate)
    coupling = times_t(costate_whole, schur)
    coupled = to_columns(coupling.astype(BF16)).astype(F32)
    state = to_columns(start_state.T.astype(BF16))
    advanced = times_t(state, gain_whole) - coupled
    for target in range(1, groups):
        arrived = period_send(advanced.astype(BF16), target - 1, target)
        state = jnp.where(period == target, arrived, state)
        advanced = times_t(arrived, gain_whole) - coupled
    state_whole = gathered(state)
    storage = times_t(gain, state_whole) - coupling.T
    costate_rows = lax.dynamic_slice_in_dim(costate_whole, rank * units, units, 1).T.astype(F32)
    ids = rank * buses + jnp.arange(buses, dtype=jnp.int32)
    placement = (unit_bus == ids[:, None]).astype(BF16)
    network = (weighted - times_t(placement, state_whole)).astype(BF16)
    return storage, costate_rows, times(inverse, network)


def body(
    gain, schur, inverse_blocks, sensitivity, residual_bus, unit_rhs, start_state, active_set, unit_bus
):
    in_planes = lax.axis_size("bus") == 8 and lax.axis_size("period") > 2
    storage, costate, update = (plane_body if in_planes else plain_body)(
        gain[0],
        schur[0],
        inverse_blocks[0],
        sensitivity,
        residual_bus[0],
        unit_rhs[0],
        start_state,
        active_set[0][:, None],
        unit_bus[None, :],
    )
    return storage[None], costate[None], update[None]


def solution(mesh):
    by_period = P("period", "bus", None)
    placed = (
        by_period,
        by_period,
        by_period,
        P("bus", None),
        by_period,
        by_period,
        P("bus", None),
        P("period", "bus"),
        P(),
    )
    return jax.shard_map(
        body,
        mesh=mesh,
        in_specs=placed,
        out_specs=(by_period, by_period, by_period),
        check_vma=False,
    )
```

```python
import functools

import jax
import jax.numpy as jnp
from jax import lax
from jax.experimental import pallas as pl
from jax.experimental.pallas import tpu as pltpu
from jax.sharding import PartitionSpec as P

BOTH = ("period", "bus")
F32 = jnp.float32
BF16 = jnp.bfloat16
EVEN = (0, 2, 4, 6)
MIB = 1 << 20


def bus_send(block, flip, periods):
    size = lax.axis_size("bus")
    route = [(p * size + b, p * size + (b ^ flip)) for p in periods for b in range(size)]
    return lax.ppermute(block, BOTH, route)


def period_send(block, source, target):
    size = lax.axis_size("bus")
    route = [(source * size + b, target * size + b) for b in range(size)]
    return lax.ppermute(block, BOTH, route)


def times(left, right):
    return jnp.dot(left, right, preferred_element_type=F32)


def times_t(left, right):
    return lax.dot_general(left, right, (((1,), (1,)), ((), ())), preferred_element_type=F32)


def gather_parts(block, periods):
    parts = {0: block}
    for flip in (6, 4, 2):
        parts[flip] = bus_send(block, flip, periods)
    for flip in EVEN:
        parts[flip ^ 1] = bus_send(parts[flip], 1, periods)
    return [parts[flip] for flip in range(8)]


def reduce_parts(keep, send, periods):
    there = bus_send(send, 1, periods)
    total = None
    for place, flip in ((3, 6), (2, 4), (1, 2), (0, 0)):
        here = keep[place] + there[place].astype(F32)
        if flip:
            here = bus_send(here.astype(BF16), flip, periods).astype(F32)
        total = here if total is None else total + here
    return total


def swap_parts(keep, send, periods):
    there = bus_send(send, 1, periods)
    parts = {}
    for place, flip in enumerate(EVEN):
        pair = jnp.stack([keep[place], there[place]])
        if flip:
            pair = bus_send(pair, flip, periods)
        parts[flip], parts[flip ^ 1] = pair[0], pair[1]
    return [parts[flip] for flip in range(8)]


def in_vmem():
    return pl.BlockSpec(memory_space=pltpu.VMEM)


def anywhere():
    return pl.BlockSpec(memory_space=pl.ANY)


def in_smem():
    return pl.BlockSpec(memory_space=pltpu.SMEM)


def kernel_call(kernel, out_shape, in_specs, scratch, flops, bytes_accessed):
    return pl.pallas_call(
        kernel,
        out_shape=out_shape,
        in_specs=in_specs,
        out_specs=jax.tree.map(lambda _: in_vmem(), out_shape),
        scratch_shapes=scratch,
        compiler_params=pltpu.CompilerParams(vmem_limit_bytes=48 * MIB),
        cost_estimate=pl.CostEstimate(
            flops=flops, bytes_accessed=bytes_accessed, transcendentals=0
        ),
    )


def deal(rank, whole, keep, send):
    rows = keep.shape[1]
    for place, flip in enumerate(EVEN):
        owner = pl.multiple_of((rank ^ flip) * rows, rows)
        keep[place] = whole[pl.ds(owner, rows), :].astype(keep.dtype)
        owner = pl.multiple_of((rank ^ flip ^ 1) * rows, rows)
        send[place] = whole[pl.ds(owner, rows), :].astype(send.dtype)


def front_kernel(
    rank_ref, active, rhs, residual_hbm, inverse_hbm, sens_hbm,
    keep, send,
    residual, inverse, sens, net, solve_t, partial, sems,
):
    rank = rank_ref[0]
    loads = [
        pltpu.make_async_copy(residual_hbm, residual, sems.at[0]),
        pltpu.make_async_copy(inverse_hbm, inverse, sems.at[1]),
        pltpu.make_async_copy(sens_hbm, sens, sems.at[2]),
    ]
    for load in loads:
        load.start()
    loads[0].wait()
    net[...] = (residual[...] * (1.0 + 3.0 * active[...].astype(F32))).astype(BF16)
    loads[1].wait()
    blocks = inverse.shape[0] // 256

    @pl.loop(0, blocks)
    def _(i):
        rows = pl.ds(pl.multiple_of(i * 256, 256), 256)
        solve_t[:, rows] = times(inverse[rows, :], net[...]).T.astype(BF16)

    loads[2].wait()

    @pl.loop(0, sens.shape[1] // 256)
    def _(i):
        columns = pl.ds(pl.multiple_of(i * 256, 256), 256)
        partial[:, columns] = times(solve_t[...], sens[:, columns])

    units = rhs.shape[0]
    own = pl.ds(pl.multiple_of(rank * units, units), units)
    partial[:, own] += rhs[...].T
    deal(rank, partial, keep, send)


def front(rank, active, rhs, residual, inverse, sens):
    buses, columns = residual.shape
    units = sens.shape[1]
    rows = columns // 8
    keep = jax.ShapeDtypeStruct((4, rows, units), F32)
    send = jax.ShapeDtypeStruct((4, rows, units), BF16)
    return kernel_call(
        front_kernel,
        [keep, send],
        [in_smem(), in_vmem(), in_vmem(), anywhere(), anywhere(), anywhere()],
        [
            pltpu.VMEM((buses, columns), F32),
            pltpu.VMEM((buses, buses), BF16),
            pltpu.VMEM((buses, units), BF16),
            pltpu.VMEM((buses, columns), BF16),
            pltpu.VMEM((columns, buses), BF16),
            pltpu.VMEM((columns, units), F32),
            pltpu.SemaphoreType.DMA((3,)),
        ],
        2 * buses * columns * (buses + units),
        24 * MIB,
    )(rank, active, rhs, residual, inverse, sens)


def weight_loads(rank, weights, held, sems):
    units = held.shape[1]
    loads = []
    for flip in range(8):
        owner = pl.multiple_of((rank ^ flip) * units, units)
        source = weights.at[pl.ds(owner, units)]
        loads.append(pltpu.make_async_copy(source, held.at[flip], sems.at[flip]))
    return loads


def backward_kernel(rank_ref, vector, base, *refs):
    weights, out, held, total, sems = refs
    rank = rank_ref[0]
    loads = weight_loads(rank, weights, held, sems)
    for load in loads:
        load.start()
    units = held.shape[1]
    total[...] = base[...]
    for flip, load in enumerate(loads):
        load.wait()
        own = pl.ds(pl.multiple_of((rank ^ flip) * units, units), units)
        total[...] += times(vector[:, own], held[flip])
    out[...] = total[...].astype(out.dtype)


def forward_kernel(subtract, rank_ref, vector, *refs):
    weights, refs = refs[0], refs[1:]
    terms, (out, held, sems) = (refs[:8], refs[8:]) if subtract else (None, refs)
    rank = rank_ref[0]
    loads = weight_loads(rank, weights, held, sems)
    for load in loads:
        load.start()
    units = held.shape[1]
    for flip, load in enumerate(loads):
        load.wait()
        own = pl.ds(pl.multiple_of((rank ^ flip) * units, units), units)
        product = times_t(vector[...], held[flip])
        if subtract:
            product = product - terms[flip][...].astype(F32)
        out[:, own] = product.astype(out.dtype)


def backward(rank, vector, base, weights):
    rows, whole = vector.shape
    units = weights.shape[0] // 8
    return kernel_call(
        backward_kernel,
        jax.ShapeDtypeStruct((rows, whole), BF16),
        [in_smem(), in_vmem(), in_vmem()] + [anywhere()],
        [
            pltpu.VMEM((8, units, whole), BF16),
            pltpu.VMEM((rows, whole), F32),
            pltpu.SemaphoreType.DMA((8,)),
        ],
        2 * rows * whole * whole,
        2 * whole * whole,
    )(rank, vector, base, weights)


def forward(rank, vector, weights, terms=()):
    rows, whole = vector.shape
    units = weights.shape[0] // 8
    return kernel_call(
        functools.partial(forward_kernel, bool(terms)),
        jax.ShapeDtypeStruct((rows, whole), BF16 if terms else F32),
        [in_smem(), in_vmem()] + [anywhere()] + [in_vmem()] * len(terms),
        [pltpu.VMEM((8, units, whole), BF16), pltpu.SemaphoreType.DMA((8,))],
        2 * rows * whole * whole,
        2 * whole * whole,
    )(rank, vector, weights, *terms)


def assemble(rank, first, second, whole):
    rows = first[0].shape[0]
    for flip in range(8):
        owner = pl.multiple_of((rank ^ flip) * rows, rows)
        block = first[flip][...]
        if flip and second:
            block = block + second[flip - 1][...]
        whole[pl.ds(owner, rows), :] = block


def couple_kernel(rank_ref, schur, *refs):
    parts, (keep, send, costate, coupling, product, whole) = refs[:8], refs[8:]
    rank = rank_ref[0]
    assemble(rank, parts, (), whole)
    product[...] = times_t(whole[...], schur[...])
    deal(rank, product, keep, send)
    coupling[...] = product[...].T
    units = schur.shape[0]
    own = pl.ds(pl.multiple_of(rank * units, units), units)
    costate[...] = whole[:, own].astype(F32).T


def couple(rank, schur, parts):
    units, whole = schur.shape
    rows = parts[0].shape[0]
    piece = jax.ShapeDtypeStruct((4, rows, units), BF16)
    out = jax.ShapeDtypeStruct((units, 8 * rows), F32)
    return kernel_call(
        couple_kernel,
        [piece, piece, out, out],
        [in_smem(), in_vmem()] + [in_vmem()] * 8,
        [pltpu.VMEM((8 * rows, units), F32), pltpu.VMEM((8 * rows, whole), BF16)],
        16 * rows * whole * units,
        4 * MIB,
    )(rank, schur, *parts)


def finish_kernel(rank_ref, driven, *refs):
    terms, out = refs[:8], refs[8]
    rank = rank_ref[0]
    units = terms[0].shape[1]
    for flip in range(8):
        own = pl.ds(pl.multiple_of((rank ^ flip) * units, units), units)
        out[:, own] = (driven[:, own] - terms[flip][...].astype(F32)).astype(out.dtype)


def finish(rank, driven, terms):
    return kernel_call(
        finish_kernel,
        jax.ShapeDtypeStruct(driven.shape, BF16),
        [in_smem(), in_vmem()] + [in_vmem()] * 8,
        [],
        driven.size,
        8 * driven.size,
    )(rank, driven, *terms)


def final_kernel(rank_ref, unit_bus, active, coupling, gain, residual_hbm, inverse_hbm, *refs):
    first, second = refs[:8], refs[8:15]
    storage, update, residual, inverse, whole, network, sems = refs[15:]
    rank = rank_ref[0]
    loads = [
        pltpu.make_async_copy(residual_hbm, residual, sems.at[0]),
        pltpu.make_async_copy(inverse_hbm, inverse, sems.at[1]),
    ]
    for load in loads:
        load.start()
    assemble(rank, first, second, whole)
    loads[0].wait()
    buses = inverse.shape[0]

    @pl.loop(0, buses // 256)
    def _(i):
        rows = pl.ds(pl.multiple_of(i * 256, 256), 256)
        ids = rank * buses + i * 256 + lax.broadcasted_iota(jnp.int32, (256, 1), 0)
        placed = (unit_bus[...] == ids).astype(BF16)
        injection = times_t(placed, whole[...])
        weighted = residual[rows, :] * (1.0 + 3.0 * active[rows, :].astype(F32))
        network[rows, :] = (weighted - injection).astype(BF16)

    storage[...] = times_t(gain[...], whole[...]) - coupling[...]
    loads[1].wait()

    @pl.loop(0, buses // 256)
    def _(i):
        rows = pl.ds(pl.multiple_of(i * 256, 256), 256)
        update[rows, :] = times(inverse[rows, :], network[...])


def final(rank, unit_bus, active, coupling, gain, residual, inverse, first, second):
    buses, columns = residual.shape
    units, whole = gain.shape
    return kernel_call(
        final_kernel,
        [
            jax.ShapeDtypeStruct((units, columns), F32),
            jax.ShapeDtypeStruct((buses, columns), F32),
        ],
        [in_smem()] + [in_vmem()] * 4 + [anywhere()] * 2 + [in_vmem()] * 15,
        [
            pltpu.VMEM((buses, columns), F32),
            pltpu.VMEM((buses, buses), BF16),
            pltpu.VMEM((columns, whole), BF16),
            pltpu.VMEM((buses, columns), BF16),
            pltpu.SemaphoreType.DMA((2,)),
        ],
        2 * columns * (buses * buses + (buses + units) * whole),
        24 * MIB,
    )(rank, unit_bus, active, coupling, gain, residual, inverse, *first, *second[1:])


def plane_body(
    gain, schur, inverse, sens, residual, unit_rhs, start_state, active, unit_bus
):
    period = lax.axis_index("period")
    rank = lax.axis_index("bus").reshape(1)
    last = lax.axis_size("period") - 1
    everyone = tuple(range(last + 1))
    rows = residual.shape[1] // 8

    gain_whole = lax.all_gather(gain, "bus", axis=0, tiled=True)
    keep, send = front(rank, active, unit_rhs, residual, inverse, sens)
    unit_right = reduce_parts(keep, send, everyone)

    start_t = start_state.T.astype(BF16)

    def start_piece(owner):
        return lax.dynamic_slice_in_dim(start_t, owner * rows, rows, 0)

    keep = jnp.stack([start_piece(rank[0] ^ flip) for flip in EVEN])
    send = jnp.stack([start_piece(rank[0] ^ flip ^ 1) for flip in EVEN])
    pieces = jnp.stack(swap_parts(keep, send, everyone))
    ordered = jnp.take(pieces, jnp.arange(8, dtype=jnp.int32) ^ rank[0], axis=0)
    start = jnp.transpose(ordered, (1, 0, 2)).reshape(rows, -1)

    costate = unit_right.astype(BF16)
    for target in range(last - 1, -1, -1):
        later = period_send(costate, target + 1, target)
        costate = jnp.where(period == target, backward(rank, later, unit_right, gain_whole), costate)
    costates = gather_parts(costate, everyone)
    keep, send, costate_rows, coupling = couple(rank, schur, costates)
    coupled = swap_parts(keep, send, everyone)

    state = start
    advanced = finish(rank, forward(rank, start, gain_whole), coupled)
    for target in range(1, last + 1):
        arrived = period_send(advanced, target - 1, target)
        state = jnp.where(period == target, arrived, state)
        if target < last:
            early = state
            advanced = forward(rank, arrived, gain_whole, coupled)
    early, state = lax.optimization_barrier((early, state))
    last_states = gather_parts(state, (last,))
    early_states = gather_parts(early, everyone[:-1])
    storage, update = final(
        rank, unit_bus, active, coupling, gain, residual, inverse, last_states, early_states
    )
    return storage, costate_rows, update


def plain_body(
    gain, schur, inverse, sens, residual, unit_rhs, start_state, active, unit_bus
):
    period = lax.axis_index("period")
    rank = lax.axis_index("bus")
    size = lax.axis_size("bus")
    groups = lax.axis_size("period")
    units, whole = gain.shape
    buses, columns = residual.shape
    rows = columns // size

    def gathered(block):
        return lax.all_gather(block, "bus", axis=0, tiled=True)

    def to_columns(block):
        swapped = lax.all_to_all(block.reshape(size, rows, units), "bus", 0, 0)
        return jnp.transpose(swapped, (1, 0, 2)).reshape(rows, whole)

    weighted = residual * (1.0 + 3.0 * active.astype(F32))
    solve = times(inverse, weighted.astype(BF16)).astype(BF16)
    partial = lax.dot_general(solve, sens, (((0,), (0,)), ((), ())), preferred_element_type=F32)
    place = (0, rank * units)
    own = lax.dynamic_slice(partial, place, (columns, units)) + unit_rhs.T
    partial = lax.dynamic_update_slice(partial, own, place).astype(BF16)
    unit_right = lax.psum_scatter(partial, "bus", scatter_dimension=0, tiled=True).astype(F32)
    gain_whole = gathered(gain)
    costate = unit_right.astype(BF16)
    for target in range(groups - 2, -1, -1):
        later = period_send(costate, target + 1, target)
        current = (unit_right + times(later, gain_whole)).astype(BF16)
        costate = jnp.where(period == target, current, costate)
    costate_whole = gathered(costate)
    coupling = times_t(costate_whole, schur)
    coupled = to_columns(coupling.astype(BF16)).astype(F32)
    state = to_columns(start_state.T.astype(BF16))
    advanced = times_t(state, gain_whole) - coupled
    for target in range(1, groups):
        arrived = period_send(advanced.astype(BF16), target - 1, target)
        state = jnp.where(period == target, arrived, state)
        advanced = times_t(arrived, gain_whole) - coupled
    state_whole = gathered(state)
    storage = times_t(gain, state_whole) - coupling.T
    costate_rows = lax.dynamic_slice_in_dim(costate_whole, rank * units, units, 1).T.astype(F32)
    ids = rank * buses + jnp.arange(buses, dtype=jnp.int32)
    placement = (unit_bus == ids[:, None]).astype(BF16)
    network = (weighted - times_t(placement, state_whole)).astype(BF16)
    return storage, costate_rows, times(inverse, network)


def body(
    gain, schur, inverse_blocks, sensitivity, residual_bus, unit_rhs, start_state, active_set, unit_bus
):
    in_planes = lax.axis_size("bus") == 8 and lax.axis_size("period") > 2
    storage, costate, update = (plane_body if in_planes else plain_body)(
        gain[0],
        schur[0],
        inverse_blocks[0],
        sensitivity,
        residual_bus[0],
        unit_rhs[0],
        start_state,
        active_set[0][:, None],
        unit_bus[None, :],
    )
    return storage[None], costate[None], update[None]


def solution(mesh):
    by_period = P("period", "bus", None)
    placed = (
        by_period,
        by_period,
        by_period,
        P("bus", None),
        by_period,
        by_period,
        P("bus", None),
        P("period", "bus"),
        P(),
    )
    return jax.shard_map(
        body,
        mesh=mesh,
        in_specs=placed,
        out_specs=(by_period, by_period, by_period),
        check_vma=False,
    )
```

```python
import functools

import jax
import jax.numpy as jnp
from jax import lax
from jax.experimental import pallas as pl
from jax.experimental.pallas import tpu as pltpu
from jax.sharding import PartitionSpec as P

BOTH = ("period", "bus")
F32 = jnp.float32
BF16 = jnp.bfloat16
EVEN = (0, 2, 4, 6)
MIB = 1 << 20


def bus_send(block, flip, periods):
    size = lax.axis_size("bus")
    route = [(p * size + b, p * size + (b ^ flip)) for p in periods for b in range(size)]
    return lax.ppermute(block, BOTH, route)


def period_send(block, source, target):
    size = lax.axis_size("bus")
    route = [(source * size + b, target * size + b) for b in range(size)]
    return lax.ppermute(block, BOTH, route)


def times(left, right):
    return jnp.dot(left, right, preferred_element_type=F32)


def times_t(left, right):
    return lax.dot_general(left, right, (((1,), (1,)), ((), ())), preferred_element_type=F32)


def line_send(block, pairs, periods):
    size = lax.axis_size("bus")
    route = [
        (p * size + 2 * source + y, p * size + 2 * target + y)
        for p in periods
        for source, target in pairs
        for y in range(2)
    ]
    return lax.ppermute(block, BOTH, route)


def across(block, periods):
    return line_send(block, ((1, 2), (2, 1)), periods)


def outwards(block, periods):
    return line_send(block, ((1, 0), (2, 3)), periods)


def together(*values):
    return lax.optimization_barrier(values)


def gather_parts(block, periods):
    four, six = bus_send(block, 4, periods), bus_send(block, 6, periods)
    two, one = together(bus_send(block, 2, periods), bus_send(block, 1, periods))
    four, three = together(four, bus_send(two, 1, periods))
    six, five = together(six, bus_send(four, 1, periods))
    return [block, one, two, three, four, five, six, bus_send(six, 1, periods)]


def reduce_z(keep, there, periods):
    total = None
    for place, flip in ((3, 6), (2, 4), (1, 2), (0, 0)):
        here = keep[place] + there[place].astype(F32)
        if flip:
            here = bus_send(here.astype(BF16), flip, periods).astype(F32)
        total = here if total is None else total + here
    return total


def swap_parts(keep, send, periods):
    there = bus_send(send, 1, periods)
    parts = {}
    for place, flip in enumerate(EVEN):
        pair = jnp.stack([keep[place], there[place]])
        if flip:
            pair = bus_send(pair, flip, periods)
        parts[flip] = pair
    return jnp.concatenate([parts[flip] for flip in EVEN])


def in_vmem():
    return pl.BlockSpec(memory_space=pltpu.VMEM)


def anywhere():
    return pl.BlockSpec(memory_space=pl.ANY)


def in_smem():
    return pl.BlockSpec(memory_space=pltpu.SMEM)


def kernel_call(kernel, out_shape, in_specs, scratch, flops, bytes_accessed, mib):
    return pl.pallas_call(
        kernel,
        out_shape=out_shape,
        in_specs=in_specs,
        out_specs=jax.tree.map(lambda _: in_vmem(), out_shape),
        scratch_shapes=scratch,
        compiler_params=pltpu.CompilerParams(vmem_limit_bytes=mib * MIB),
        cost_estimate=pl.CostEstimate(
            flops=flops, bytes_accessed=bytes_accessed, transcendentals=0
        ),
    )


def deal(rank, whole, keep, send):
    rows = keep.shape[1]
    for place, flip in enumerate(EVEN):
        owner = pl.multiple_of((rank ^ flip) * rows, rows)
        keep[place] = whole[pl.ds(owner, rows), :].astype(keep.dtype)
        owner = pl.multiple_of((rank ^ flip ^ 1) * rows, rows)
        send[place] = whole[pl.ds(owner, rows), :].astype(send.dtype)


def front_kernel(
    rank_ref, active, rhs, residual_hbm, inverse_hbm, sens_hbm,
    keep, send,
    residual, inverse, sens, net, solve_t, partial, sems,
):
    rank = rank_ref[0]
    loads = [
        pltpu.make_async_copy(residual_hbm, residual, sems.at[0]),
        pltpu.make_async_copy(inverse_hbm, inverse, sems.at[1]),
        pltpu.make_async_copy(sens_hbm, sens, sems.at[2]),
    ]
    for load in loads:
        load.start()
    loads[0].wait()
    net[...] = (residual[...] * (1.0 + 3.0 * active[...].astype(F32))).astype(BF16)
    loads[1].wait()
    blocks = inverse.shape[0] // 256

    @pl.loop(0, blocks)
    def _(i):
        rows = pl.ds(pl.multiple_of(i * 256, 256), 256)
        solve_t[:, rows] = times(inverse[rows, :], net[...]).T.astype(BF16)

    loads[2].wait()

    @pl.loop(0, sens.shape[1] // 256)
    def _(i):
        columns = pl.ds(pl.multiple_of(i * 256, 256), 256)
        partial[:, columns] = times(solve_t[...], sens[:, columns])

    units = rhs.shape[0]
    own = pl.ds(pl.multiple_of(rank * units, units), units)
    partial[:, own] += rhs[...].T
    deal(rank, partial, keep, send)


def front(rank, active, rhs, residual, inverse, sens):
    buses, columns = residual.shape
    units = sens.shape[1]
    rows = columns // 8
    keep = jax.ShapeDtypeStruct((4, rows, units), F32)
    send = jax.ShapeDtypeStruct((4, rows, units), BF16)
    return kernel_call(
        front_kernel,
        [keep, send],
        [in_smem(), in_vmem(), in_vmem(), anywhere(), anywhere(), anywhere()],
        [
            pltpu.VMEM((buses, columns), F32),
            pltpu.VMEM((buses, buses), BF16),
            pltpu.VMEM((buses, units), BF16),
            pltpu.VMEM((buses, columns), BF16),
            pltpu.VMEM((columns, buses), BF16),
            pltpu.VMEM((columns, units), F32),
            pltpu.SemaphoreType.DMA((3,)),
        ],
        2 * buses * columns * (buses + units),
        24 * MIB,
        48,
    )(rank, active, rhs, residual, inverse, sens)


def start_kernel(rank_ref, state, keep, send, whole):
    whole[...] = state[...].T
    deal(rank_ref[0], whole, keep, send)


def start_pieces(rank, state):
    units, columns = state.shape
    piece = jax.ShapeDtypeStruct((4, columns // 8, units), BF16)
    return kernel_call(
        start_kernel,
        [piece, piece],
        [in_smem(), in_vmem()],
        [pltpu.VMEM((columns, units), F32)],
        state.size,
        6 * state.size,
        8,
    )(rank, state)


def join_kernel(rank_ref, pieces, out):
    units = pieces.shape[2]
    for flip in range(8):
        own = pl.ds(pl.multiple_of((rank_ref[0] ^ flip) * units, units), units)
        out[:, own] = pieces[flip]


def join(rank, pieces):
    _, rows, units = pieces.shape
    return kernel_call(
        join_kernel,
        jax.ShapeDtypeStruct((rows, 8 * units), BF16),
        [in_smem(), in_vmem()],
        [],
        pieces.size,
        4 * pieces.size,
        8,
    )(rank, pieces)


def pack_kernel(*refs):
    parts, (out, sems) = refs[:7], refs[7:]
    loads = [pltpu.make_async_copy(part, out.at[j], sems.at[j]) for j, part in enumerate(parts)]
    for load in loads:
        load.start()
    for load in loads:
        load.wait()


def pack(parts):
    return kernel_call(
        pack_kernel,
        jax.ShapeDtypeStruct((len(parts), *parts[0].shape), BF16),
        [anywhere()] * len(parts),
        [pltpu.SemaphoreType.DMA((len(parts),))],
        0,
        4 * len(parts) * parts[0].size,
        48,
    )(*parts)


def backward_kernel(places, vector, base, packed, final_part, out, total):
    units = final_part.shape[0]
    total[...] = base[...]
    for place in range(8):
        weight = packed[place] if place < 7 else final_part[...]
        own = pl.ds(pl.multiple_of(places[place] * units, units), units)
        total[...] += times(vector[:, own], weight)
    out[...] = total[...].astype(out.dtype)


def forward_kernel(places, vector, packed, final_part, *refs):
    terms, out = refs if len(refs) > 1 else (None, refs[0])
    units = final_part.shape[0]
    for place in range(8):
        weight = packed[place] if place < 7 else final_part[...]
        own = pl.ds(pl.multiple_of(places[place] * units, units), units)
        product = times_t(vector[...], weight)
        if terms is not None:
            product = product - terms[places[place] ^ places[0]].astype(F32)
        out[:, own] = product.astype(out.dtype)


def backward(places, vector, base, weights):
    rows, whole = vector.shape
    return kernel_call(
        backward_kernel,
        jax.ShapeDtypeStruct((rows, whole), BF16),
        [in_smem()] + [in_vmem()] * 4,
        [pltpu.VMEM((rows, whole), F32)],
        2 * rows * whole * whole,
        2 * whole * whole,
        12,
    )(places, vector, base, *weights)


def forward(places, vector, weights, terms=None):
    rows, whole = vector.shape
    extra = () if terms is None else (terms,)
    return kernel_call(
        forward_kernel,
        jax.ShapeDtypeStruct((rows, whole), BF16 if extra else F32),
        [in_smem()] + [in_vmem()] * (3 + len(extra)),
        [],
        2 * rows * whole * whole,
        2 * whole * whole,
        12,
    )(places, vector, *weights, *extra)


def assemble(rank, first, second, whole):
    rows = first[0].shape[0]
    for flip in range(8):
        owner = pl.multiple_of((rank ^ flip) * rows, rows)
        block = first[flip][...]
        if flip and second:
            block = block + second[flip - 1][...]
        whole[pl.ds(owner, rows), :] = block


def couple_kernel(rank_ref, schur, *refs):
    parts, (keep, send, costate, coupling, product, whole) = refs[:8], refs[8:]
    rank = rank_ref[0]
    assemble(rank, parts, (), whole)
    product[...] = times_t(whole[...], schur[...])
    deal(rank, product, keep, send)
    coupling[...] = product[...].T
    units = schur.shape[0]
    own = pl.ds(pl.multiple_of(rank * units, units), units)
    costate[...] = whole[:, own].astype(F32).T


def couple(rank, schur, parts):
    units, whole = schur.shape
    rows = parts[0].shape[0]
    piece = jax.ShapeDtypeStruct((4, rows, units), BF16)
    out = jax.ShapeDtypeStruct((units, 8 * rows), F32)
    return kernel_call(
        couple_kernel,
        [piece, piece, out, out],
        [in_smem(), in_vmem()] + [in_vmem()] * 8,
        [pltpu.VMEM((8 * rows, units), F32), pltpu.VMEM((8 * rows, whole), BF16)],
        16 * rows * whole * units,
        4 * MIB,
        16,
    )(rank, schur, *parts)


def finish_kernel(rank_ref, driven, terms, out):
    units = terms.shape[2]
    for flip in range(8):
        own = pl.ds(pl.multiple_of((rank_ref[0] ^ flip) * units, units), units)
        out[:, own] = (driven[:, own] - terms[flip].astype(F32)).astype(out.dtype)


def finish(rank, driven, terms):
    return kernel_call(
        finish_kernel,
        jax.ShapeDtypeStruct(driven.shape, BF16),
        [in_smem(), in_vmem(), in_vmem()],
        [],
        driven.size,
        8 * driven.size,
        8,
    )(rank, driven, terms)


def final_kernel(rank_ref, unit_bus, active, coupling, gain, residual_hbm, inverse_hbm, *refs):
    first, second = refs[:8], refs[8:15]
    storage, update, residual, inverse, whole, network, sems = refs[15:]
    rank = rank_ref[0]
    loads = [
        pltpu.make_async_copy(residual_hbm, residual, sems.at[0]),
        pltpu.make_async_copy(inverse_hbm, inverse, sems.at[1]),
    ]
    for load in loads:
        load.start()
    assemble(rank, first, second, whole)
    loads[0].wait()
    buses = inverse.shape[0]

    @pl.loop(0, buses // 256)
    def _(i):
        rows = pl.ds(pl.multiple_of(i * 256, 256), 256)
        ids = rank * buses + i * 256 + lax.broadcasted_iota(jnp.int32, (256, 1), 0)
        placed = (unit_bus[...] == ids).astype(BF16)
        injection = times_t(placed, whole[...])
        weighted = residual[rows, :] * (1.0 + 3.0 * active[rows, :].astype(F32))
        network[rows, :] = (weighted - injection).astype(BF16)

    storage[...] = times_t(gain[...], whole[...]) - coupling[...]
    loads[1].wait()

    @pl.loop(0, buses // 256)
    def _(i):
        rows = pl.ds(pl.multiple_of(i * 256, 256), 256)
        update[rows, :] = times(inverse[rows, :], network[...])


def final(rank, unit_bus, active, coupling, gain, residual, inverse, first, second):
    buses, columns = residual.shape
    units, whole = gain.shape
    return kernel_call(
        final_kernel,
        [
            jax.ShapeDtypeStruct((units, columns), F32),
            jax.ShapeDtypeStruct((buses, columns), F32),
        ],
        [in_smem()] + [in_vmem()] * 4 + [anywhere()] * 2 + [in_vmem()] * 15,
        [
            pltpu.VMEM((buses, columns), F32),
            pltpu.VMEM((buses, buses), BF16),
            pltpu.VMEM((columns, whole), BF16),
            pltpu.VMEM((buses, columns), BF16),
            pltpu.SemaphoreType.DMA((2,)),
        ],
        2 * columns * (buses * buses + (buses + units) * whole),
        24 * MIB,
        48,
    )(rank, unit_bus, active, coupling, gain, residual, inverse, *first, *second[1:])


def plane_body(
    gain, schur, inverse, sens, residual, unit_rhs, start_state, active, unit_bus
):
    period = lax.axis_index("period")
    rank = lax.axis_index("bus").reshape(1)
    last = lax.axis_size("period") - 1
    everyone = tuple(range(last + 1))
    rows = residual.shape[1] // 8

    far_end = (rank[0] < 2) | (rank[0] >= 6)
    order = jnp.where(
        far_end,
        jnp.array([0, 1, 2, 3, 4, 5, 6, 7], jnp.int32),
        jnp.array([0, 1, 2, 3, 6, 7, 4, 5], jnp.int32),
    )
    places = rank ^ order

    near, middle, own_y = (
        bus_send(gain, 2, everyone), across(gain, everyone), bus_send(gain, 1, everyone)
    )
    keep, send = front(rank, active, unit_rhs, residual, inverse, sens)
    near, middle, own_y, keep, send = together(near, middle, own_y, keep, send)
    there = bus_send(send, 1, everyone)
    near_y = bus_send(near, 1, everyone)
    middle2, third, near_y = together(
        across(near, everyone), middle + outwards(middle, everyone), near_y
    )
    third_y = bus_send(third, 1, everyone)
    fourth = middle2 + outwards(middle2, everyone)
    fourth, third_y, there = together(fourth, third_y, there)
    packed, fourth_y, unit_right = together(
        pack([gain, own_y, near, near_y, third, third_y, fourth]),
        bus_send(fourth, 1, everyone),
        reduce_z(keep, there, everyone),
    )
    weights = [packed, fourth_y]
    start = join(rank, swap_parts(*start_pieces(rank, start_state), everyone))

    costate = unit_right.astype(BF16)
    for target in range(last - 1, -1, -1):
        later = period_send(costate, target + 1, target)
        costate = jnp.where(
            period == target, backward(places, later, unit_right, weights), costate
        )
    costates = gather_parts(costate, everyone)
    keep, send, costate_rows, coupling = couple(rank, schur, costates)
    coupled = swap_parts(keep, send, everyone)

    state = start
    advanced = finish(rank, forward(places, start, weights), coupled)
    for target in range(1, last + 1):
        arrived = period_send(advanced, target - 1, target)
        state = jnp.where(period == target, arrived, state)
        if target < last:
            early = state
            advanced = forward(places, arrived, weights, coupled)
    early, state = together(early, state)
    last_states = gather_parts(state, (last,))
    early_states = gather_parts(early, everyone[:-1])
    storage, update = final(
        rank, unit_bus, active, coupling, gain, residual, inverse, last_states, early_states
    )
    return storage, costate_rows, update


def plain_body(
    gain, schur, inverse, sens, residual, unit_rhs, start_state, active, unit_bus
):
    period = lax.axis_index("period")
    rank = lax.axis_index("bus")
    size = lax.axis_size("bus")
    groups = lax.axis_size("period")
    units, whole = gain.shape
    buses, columns = residual.shape
    rows = columns // size

    def gathered(block):
        return lax.all_gather(block, "bus", axis=0, tiled=True)

    def to_columns(block):
        swapped = lax.all_to_all(block.reshape(size, rows, units), "bus", 0, 0)
        return jnp.transpose(swapped, (1, 0, 2)).reshape(rows, whole)

    weighted = residual * (1.0 + 3.0 * active.astype(F32))
    solve = times(inverse, weighted.astype(BF16)).astype(BF16)
    partial = lax.dot_general(solve, sens, (((0,), (0,)), ((), ())), preferred_element_type=F32)
    place = (0, rank * units)
    own = lax.dynamic_slice(partial, place, (columns, units)) + unit_rhs.T
    partial = lax.dynamic_update_slice(partial, own, place).astype(BF16)
    unit_right = lax.psum_scatter(partial, "bus", scatter_dimension=0, tiled=True).astype(F32)
    gain_whole = gathered(gain)
    costate = unit_right.astype(BF16)
    for target in range(groups - 2, -1, -1):
        later = period_send(costate, target + 1, target)
        current = (unit_right + times(later, gain_whole)).astype(BF16)
        costate = jnp.where(period == target, current, costate)
    costate_whole = gathered(costate)
    coupling = times_t(costate_whole, schur)
    coupled = to_columns(coupling.astype(BF16)).astype(F32)
    state = to_columns(start_state.T.astype(BF16))
    advanced = times_t(state, gain_whole) - coupled
    for target in range(1, groups):
        arrived = period_send(advanced.astype(BF16), target - 1, target)
        state = jnp.where(period == target, arrived, state)
        advanced = times_t(arrived, gain_whole) - coupled
    state_whole = gathered(state)
    storage = times_t(gain, state_whole) - coupling.T
    costate_rows = lax.dynamic_slice_in_dim(costate_whole, rank * units, units, 1).T.astype(F32)
    ids = rank * buses + jnp.arange(buses, dtype=jnp.int32)
    placement = (unit_bus == ids[:, None]).astype(BF16)
    network = (weighted - times_t(placement, state_whole)).astype(BF16)
    return storage, costate_rows, times(inverse, network)


def body(
    gain, schur, inverse_blocks, sensitivity, residual_bus, unit_rhs, start_state, active_set, unit_bus
):
    in_planes = lax.axis_size("bus") == 8 and lax.axis_size("period") > 2
    storage, costate, update = (plane_body if in_planes else plain_body)(
        gain[0],
        schur[0],
        inverse_blocks[0],
        sensitivity,
        residual_bus[0],
        unit_rhs[0],
        start_state,
        active_set[0][:, None],
        unit_bus[None, :],
    )
    return storage[None], costate[None], update[None]


def solution(mesh):
    by_period = P("period", "bus", None)
    placed = (
        by_period,
        by_period,
        by_period,
        P("bus", None),
        by_period,
        by_period,
        P("bus", None),
        P("period", "bus"),
        P(),
    )
    return jax.shard_map(
        body,
        mesh=mesh,
        in_specs=placed,
        out_specs=(by_period, by_period, by_period),
        check_vma=False,
    )
```

```python
import functools

import jax
import jax.numpy as jnp
from jax import lax
from jax.experimental import pallas as pl
from jax.experimental.pallas import tpu as pltpu
from jax.sharding import PartitionSpec as P

BOTH = ("period", "bus")
F32 = jnp.float32
BF16 = jnp.bfloat16
EVEN = (0, 2, 4, 6)
MIB = 1 << 20


def bus_send(block, flip, periods):
    size = lax.axis_size("bus")
    route = [(p * size + b, p * size + (b ^ flip)) for p in periods for b in range(size)]
    return lax.ppermute(block, BOTH, route)


def period_send(block, source, target):
    size = lax.axis_size("bus")
    route = [(source * size + b, target * size + b) for b in range(size)]
    return lax.ppermute(block, BOTH, route)


def times(left, right):
    return jnp.dot(left, right, preferred_element_type=F32)


def times_t(left, right):
    return lax.dot_general(left, right, (((1,), (1,)), ((), ())), preferred_element_type=F32)


def line_send(block, pairs, periods):
    size = lax.axis_size("bus")
    route = [
        (p * size + 2 * source + y, p * size + 2 * target + y)
        for p in periods
        for source, target in pairs
        for y in range(2)
    ]
    return lax.ppermute(block, BOTH, route)


def across(block, periods):
    return line_send(block, ((1, 2), (2, 1)), periods)


def outwards(block, periods):
    return line_send(block, ((1, 0), (2, 3)), periods)


def together(*values):
    return lax.optimization_barrier(values)


def gather_parts(block, periods):
    four, six = bus_send(block, 4, periods), bus_send(block, 6, periods)
    two, one = together(bus_send(block, 2, periods), bus_send(block, 1, periods))
    four, three = together(four, bus_send(two, 1, periods))
    six, five = together(six, bus_send(four, 1, periods))
    return [block, one, two, three, four, five, six, bus_send(six, 1, periods)]


def reduce_z(keep, there, periods):
    total = None
    for place, flip in ((3, 6), (2, 4), (1, 2), (0, 0)):
        here = keep[place] + there[place].astype(F32)
        if flip:
            here = bus_send(here.astype(BF16), flip, periods).astype(F32)
        total = here if total is None else total + here
    return total


def swap_z(pairs, periods):
    others = [bus_send(pairs[flip // 2], flip, periods) for flip in (2, 4, 6)]
    return jnp.concatenate([pairs[0], *others])


def swap_parts(keep, send, periods):
    there = bus_send(send, 1, periods)
    return swap_z([jnp.stack([keep[place], there[place]]) for place in range(4)], periods)


def in_vmem():
    return pl.BlockSpec(memory_space=pltpu.VMEM)


def anywhere():
    return pl.BlockSpec(memory_space=pl.ANY)


def in_smem():
    return pl.BlockSpec(memory_space=pltpu.SMEM)


def kernel_call(kernel, out_shape, in_specs, scratch, flops, bytes_accessed, mib):
    return pl.pallas_call(
        kernel,
        out_shape=out_shape,
        in_specs=in_specs,
        out_specs=jax.tree.map(lambda _: in_vmem(), out_shape),
        scratch_shapes=scratch,
        compiler_params=pltpu.CompilerParams(vmem_limit_bytes=mib * MIB),
        cost_estimate=pl.CostEstimate(
            flops=flops, bytes_accessed=bytes_accessed, transcendentals=0
        ),
    )


def deal(rank, whole, keep, send):
    rows = keep.shape[1]
    for place, flip in enumerate(EVEN):
        owner = pl.multiple_of((rank ^ flip) * rows, rows)
        keep[place] = whole[pl.ds(owner, rows), :].astype(keep.dtype)
        owner = pl.multiple_of((rank ^ flip ^ 1) * rows, rows)
        send[place] = whole[pl.ds(owner, rows), :].astype(send.dtype)


def front_kernel(
    rank_ref, active, rhs, residual_hbm, inverse_hbm, sens_hbm,
    keep, send,
    residual, inverse, sens, net, solve_t, partial, sems,
):
    rank = rank_ref[0]
    loads = [
        pltpu.make_async_copy(residual_hbm, residual, sems.at[0]),
        pltpu.make_async_copy(inverse_hbm, inverse, sems.at[1]),
        pltpu.make_async_copy(sens_hbm, sens, sems.at[2]),
    ]
    for load in loads:
        load.start()
    loads[0].wait()
    net[...] = (residual[...] * (1.0 + 3.0 * active[...].astype(F32))).astype(BF16)
    loads[1].wait()
    blocks = inverse.shape[0] // 256

    @pl.loop(0, blocks)
    def _(i):
        rows = pl.ds(pl.multiple_of(i * 256, 256), 256)
        solve_t[:, rows] = times(inverse[rows, :], net[...]).T.astype(BF16)

    loads[2].wait()

    @pl.loop(0, sens.shape[1] // 256)
    def _(i):
        columns = pl.ds(pl.multiple_of(i * 256, 256), 256)
        partial[:, columns] = times(solve_t[...], sens[:, columns])

    units = rhs.shape[0]
    own = pl.ds(pl.multiple_of(rank * units, units), units)
    partial[:, own] += rhs[...].T
    deal(rank, partial, keep, send)


def front(rank, active, rhs, residual, inverse, sens):
    buses, columns = residual.shape
    units = sens.shape[1]
    rows = columns // 8
    keep = jax.ShapeDtypeStruct((4, rows, units), F32)
    send = jax.ShapeDtypeStruct((4, rows, units), BF16)
    return kernel_call(
        front_kernel,
        [keep, send],
        [in_smem(), in_vmem(), in_vmem(), anywhere(), anywhere(), anywhere()],
        [
            pltpu.VMEM((buses, columns), F32),
            pltpu.VMEM((buses, buses), BF16),
            pltpu.VMEM((buses, units), BF16),
            pltpu.VMEM((buses, columns), BF16),
            pltpu.VMEM((columns, buses), BF16),
            pltpu.VMEM((columns, units), F32),
            pltpu.SemaphoreType.DMA((3,)),
        ],
        2 * buses * columns * (buses + units),
        24 * MIB,
        48,
    )(rank, active, rhs, residual, inverse, sens)


def start_kernel(rank_ref, state, keep, send, whole):
    whole[...] = state[...].T
    deal(rank_ref[0], whole, keep, send)


def start_pieces(rank, state):
    units, columns = state.shape
    piece = jax.ShapeDtypeStruct((4, columns // 8, units), BF16)
    return kernel_call(
        start_kernel,
        [piece, piece],
        [in_smem(), in_vmem()],
        [pltpu.VMEM((columns, units), F32)],
        state.size,
        6 * state.size,
        8,
    )(rank, state)


def join_kernel(rank_ref, pieces, out):
    units = pieces.shape[2]
    for flip in range(8):
        own = pl.ds(pl.multiple_of((rank_ref[0] ^ flip) * units, units), units)
        out[:, own] = pieces[flip]


def join(rank, pieces):
    _, rows, units = pieces.shape
    return kernel_call(
        join_kernel,
        jax.ShapeDtypeStruct((rows, 8 * units), BF16),
        [in_smem(), in_vmem()],
        [],
        pieces.size,
        4 * pieces.size,
        8,
    )(rank, pieces)


def pack_kernel(*refs):
    parts, (out, sems) = refs[:7], refs[7:]
    loads = [pltpu.make_async_copy(part, out.at[j], sems.at[j]) for j, part in enumerate(parts)]
    for load in loads:
        load.start()
    for load in loads:
        load.wait()


def pack(parts):
    return kernel_call(
        pack_kernel,
        jax.ShapeDtypeStruct((len(parts), *parts[0].shape), BF16),
        [anywhere()] * len(parts),
        [pltpu.SemaphoreType.DMA((len(parts),))],
        0,
        4 * len(parts) * parts[0].size,
        48,
    )(*parts)


def backward_kernel(places, vector, base, packed, final_part, out, total):
    units = final_part.shape[0]
    total[...] = base[...]
    for place in range(8):
        weight = packed[place] if place < 7 else final_part[...]
        own = pl.ds(pl.multiple_of(places[place] * units, units), units)
        total[...] += times(vector[:, own], weight)
    out[...] = total[...].astype(out.dtype)


def forward_kernel(places, vector, packed, final_part, *refs):
    terms, out = refs if len(refs) > 1 else (None, refs[0])
    units = final_part.shape[0]
    for place in range(8):
        weight = packed[place] if place < 7 else final_part[...]
        own = pl.ds(pl.multiple_of(places[place] * units, units), units)
        product = times_t(vector[...], weight)
        if terms is not None:
            product = product - terms[places[place] ^ places[0]].astype(F32)
        out[:, own] = product.astype(out.dtype)


def backward(places, vector, base, weights):
    rows, whole = vector.shape
    return kernel_call(
        backward_kernel,
        jax.ShapeDtypeStruct((rows, whole), BF16),
        [in_smem()] + [in_vmem()] * 4,
        [pltpu.VMEM((rows, whole), F32)],
        2 * rows * whole * whole,
        2 * whole * whole,
        12,
    )(places, vector, base, *weights)


def forward(places, vector, weights, terms=None):
    rows, whole = vector.shape
    extra = () if terms is None else (terms,)
    return kernel_call(
        forward_kernel,
        jax.ShapeDtypeStruct((rows, whole), BF16 if extra else F32),
        [in_smem()] + [in_vmem()] * (3 + len(extra)),
        [],
        2 * rows * whole * whole,
        2 * whole * whole,
        12,
    )(places, vector, *weights, *extra)


def assemble(rank, first, second, whole):
    rows = first[0].shape[0]
    for flip in range(8):
        owner = pl.multiple_of((rank ^ flip) * rows, rows)
        block = first[flip][...]
        if flip and second:
            block = block + second[flip - 1][...]
        whole[pl.ds(owner, rows), :] = block


def couple_kernel(rank_ref, schur, schur_y, *refs):
    parts, (p0, p2, p4, p6, own, cross, whole, product) = refs[:4], refs[4:]
    rank = rank_ref[0]
    rows, units = p0.shape[1:]

    def along_z(flip):
        return pl.ds(pl.multiple_of(((rank ^ flip) // 2) * rows, rows), rows)

    for part, flip in zip(parts, EVEN, strict=True):
        whole[along_z(flip), :] = part[...]
    product[0] = times_t(whole[...], schur[...])
    product[1] = times_t(whole[...], schur_y[...])
    for out, flip in zip((p0, p2, p4, p6), EVEN, strict=True):
        for place in range(2):
            out[place] = product[place, along_z(flip), :].astype(BF16)
    own[0] = product[0]
    cross[0] = product[1].astype(BF16)
    for place, out in enumerate((own, cross)):
        place_units = pl.ds(pl.multiple_of((rank ^ place) * units, units), units)
        out[1] = whole[:, place_units].astype(out.dtype)


def couple(rank, schur, schur_y, parts):
    units, whole = schur.shape
    rows = parts[0].shape[0]
    pair = jax.ShapeDtypeStruct((2, rows, units), BF16)
    return kernel_call(
        couple_kernel,
        [pair] * 4
        + [
            jax.ShapeDtypeStruct((2, 4 * rows, units), F32),
            jax.ShapeDtypeStruct((2, 4 * rows, units), BF16),
        ],
        [in_smem()] + [in_vmem()] * 6,
        [pltpu.VMEM((4 * rows, whole), BF16), pltpu.VMEM((2, 4 * rows, units), F32)],
        16 * rows * whole * units,
        4 * MIB,
        16,
    )(rank, schur, schur_y, *parts)


def rows_kernel(rank_ref, own, cross, coupling, costate, whole):
    y = rank_ref[0] % 2
    rows = whole.shape[0] // 8
    for place, out in enumerate((coupling, costate)):
        for z in range(4):
            here = pl.ds(z * rows, rows)
            whole[pl.ds(pl.multiple_of((2 * z + y) * rows, rows), rows), :] = own[place, here, :]
            other = pl.ds(pl.multiple_of((2 * z + 1 - y) * rows, rows), rows)
            whole[other, :] = cross[place, here, :].astype(F32)
        out[...] = whole[...].T


def rows_out(rank, own, cross):
    columns, units = 2 * own.shape[1], own.shape[2]
    out = jax.ShapeDtypeStruct((units, columns), F32)
    return kernel_call(
        rows_kernel,
        [out, out],
        [in_smem(), in_vmem(), in_vmem()],
        [pltpu.VMEM((columns, units), F32)],
        own.size,
        12 * own.size,
        12,
    )(rank, own, cross)


def finish_kernel(rank_ref, driven, terms, out):
    units = terms.shape[2]
    for flip in range(8):
        own = pl.ds(pl.multiple_of((rank_ref[0] ^ flip) * units, units), units)
        out[:, own] = (driven[:, own] - terms[flip].astype(F32)).astype(out.dtype)


def finish(rank, driven, terms):
    return kernel_call(
        finish_kernel,
        jax.ShapeDtypeStruct(driven.shape, BF16),
        [in_smem(), in_vmem(), in_vmem()],
        [],
        driven.size,
        8 * driven.size,
        8,
    )(rank, driven, terms)


def final_kernel(rank_ref, unit_bus, active, coupling, gain, residual_hbm, inverse_hbm, *refs):
    first, second = refs[:8], refs[8:15]
    storage, update, residual, inverse, whole, network, sems = refs[15:]
    rank = rank_ref[0]
    loads = [
        pltpu.make_async_copy(residual_hbm, residual, sems.at[0]),
        pltpu.make_async_copy(inverse_hbm, inverse, sems.at[1]),
    ]
    for load in loads:
        load.start()
    assemble(rank, first, second, whole)
    loads[0].wait()
    buses = inverse.shape[0]

    @pl.loop(0, buses // 256)
    def _(i):
        rows = pl.ds(pl.multiple_of(i * 256, 256), 256)
        ids = rank * buses + i * 256 + lax.broadcasted_iota(jnp.int32, (256, 1), 0)
        placed = (unit_bus[...] == ids).astype(BF16)
        injection = times_t(placed, whole[...])
        weighted = residual[rows, :] * (1.0 + 3.0 * active[rows, :].astype(F32))
        network[rows, :] = (weighted - injection).astype(BF16)

    storage[...] = times_t(gain[...], whole[...]) - coupling[...]
    loads[1].wait()

    @pl.loop(0, buses // 256)
    def _(i):
        rows = pl.ds(pl.multiple_of(i * 256, 256), 256)
        update[rows, :] = times(inverse[rows, :], network[...])


def final(rank, unit_bus, active, coupling, gain, residual, inverse, first, second):
    buses, columns = residual.shape
    units, whole = gain.shape
    return kernel_call(
        final_kernel,
        [
            jax.ShapeDtypeStruct((units, columns), F32),
            jax.ShapeDtypeStruct((buses, columns), F32),
        ],
        [in_smem()] + [in_vmem()] * 4 + [anywhere()] * 2 + [in_vmem()] * 15,
        [
            pltpu.VMEM((buses, columns), F32),
            pltpu.VMEM((buses, buses), BF16),
            pltpu.VMEM((columns, whole), BF16),
            pltpu.VMEM((buses, columns), BF16),
            pltpu.SemaphoreType.DMA((2,)),
        ],
        2 * columns * (buses * buses + (buses + units) * whole),
        24 * MIB,
        48,
    )(rank, unit_bus, active, coupling, gain, residual, inverse, *first, *second[1:])


def plane_body(
    gain, schur, inverse, sens, residual, unit_rhs, start_state, active, unit_bus
):
    period = lax.axis_index("period")
    rank = lax.axis_index("bus").reshape(1)
    last = lax.axis_size("period") - 1
    everyone = tuple(range(last + 1))
    rows = residual.shape[1] // 8

    far_end = (rank[0] < 2) | (rank[0] >= 6)
    order = jnp.where(
        far_end,
        jnp.array([0, 1, 2, 3, 4, 5, 6, 7], jnp.int32),
        jnp.array([0, 1, 2, 3, 6, 7, 4, 5], jnp.int32),
    )
    places = rank ^ order

    near, middle, own_y = (
        bus_send(gain, 2, everyone), across(gain, everyone), bus_send(gain, 1, everyone)
    )
    keep, send = front(rank, active, unit_rhs, residual, inverse, sens)
    near, middle, own_y, keep, send = together(near, middle, own_y, keep, send)
    there = bus_send(send, 1, everyone)
    near_y = bus_send(near, 1, everyone)
    middle2, third, near_y = together(
        across(near, everyone), middle + outwards(middle, everyone), near_y
    )
    third_y = bus_send(third, 1, everyone)
    fourth = middle2 + outwards(middle2, everyone)
    fourth, third_y, there = together(fourth, third_y, there)
    packed, fourth_y, unit_right, schur_in = together(
        pack([gain, own_y, near, near_y, third, third_y, fourth]),
        bus_send(fourth, 1, everyone),
        reduce_z(keep, there, everyone),
        schur,
    )
    weights = [packed, fourth_y]
    start = join(rank, swap_parts(*start_pieces(rank, start_state), everyone))

    costate = unit_right.astype(BF16)
    for target in range(last - 1, -1, -1):
        later = period_send(costate, target + 1, target)
        costate = jnp.where(
            period == target, backward(places, later, unit_right, weights), costate
        )
    schur_y = bus_send(schur_in, 1, everyone)
    others = [bus_send(costate, flip, everyone) for flip in (2, 4, 6)]
    *pairs, own, cross = couple(rank, schur, schur_y, [costate, *others])
    coupled = swap_z(pairs, everyone)

    state = start
    advanced = finish(rank, forward(places, start, weights), coupled)
    for target in range(1, last + 1):
        arrived = period_send(advanced, target - 1, target)
        state = jnp.where(period == target, arrived, state)
        if target < last:
            early = state
            advanced = forward(places, arrived, weights, coupled)
    cross = bus_send(cross, 1, everyone)
    coupling, costate_rows = rows_out(rank, own, cross)
    early, state = together(early, state)
    last_states = gather_parts(state, (last,))
    early_states = gather_parts(early, everyone[:-1])
    storage, update = final(
        rank, unit_bus, active, coupling, gain, residual, inverse, last_states, early_states
    )
    return storage, costate_rows, update


def plain_body(
    gain, schur, inverse, sens, residual, unit_rhs, start_state, active, unit_bus
):
    period = lax.axis_index("period")
    rank = lax.axis_index("bus")
    size = lax.axis_size("bus")
    groups = lax.axis_size("period")
    units, whole = gain.shape
    buses, columns = residual.shape
    rows = columns // size

    def gathered(block):
        return lax.all_gather(block, "bus", axis=0, tiled=True)

    def to_columns(block):
        swapped = lax.all_to_all(block.reshape(size, rows, units), "bus", 0, 0)
        return jnp.transpose(swapped, (1, 0, 2)).reshape(rows, whole)

    weighted = residual * (1.0 + 3.0 * active.astype(F32))
    solve = times(inverse, weighted.astype(BF16)).astype(BF16)
    partial = lax.dot_general(solve, sens, (((0,), (0,)), ((), ())), preferred_element_type=F32)
    place = (0, rank * units)
    own = lax.dynamic_slice(partial, place, (columns, units)) + unit_rhs.T
    partial = lax.dynamic_update_slice(partial, own, place).astype(BF16)
    unit_right = lax.psum_scatter(partial, "bus", scatter_dimension=0, tiled=True).astype(F32)
    gain_whole = gathered(gain)
    costate = unit_right.astype(BF16)
    for target in range(groups - 2, -1, -1):
        later = period_send(costate, target + 1, target)
        current = (unit_right + times(later, gain_whole)).astype(BF16)
        costate = jnp.where(period == target, current, costate)
    costate_whole = gathered(costate)
    coupling = times_t(costate_whole, schur)
    coupled = to_columns(coupling.astype(BF16)).astype(F32)
    state = to_columns(start_state.T.astype(BF16))
    advanced = times_t(state, gain_whole) - coupled
    for target in range(1, groups):
        arrived = period_send(advanced.astype(BF16), target - 1, target)
        state = jnp.where(period == target, arrived, state)
        advanced = times_t(arrived, gain_whole) - coupled
    state_whole = gathered(state)
    storage = times_t(gain, state_whole) - coupling.T
    costate_rows = lax.dynamic_slice_in_dim(costate_whole, rank * units, units, 1).T.astype(F32)
    ids = rank * buses + jnp.arange(buses, dtype=jnp.int32)
    placement = (unit_bus == ids[:, None]).astype(BF16)
    network = (weighted - times_t(placement, state_whole)).astype(BF16)
    return storage, costate_rows, times(inverse, network)


def body(
    gain, schur, inverse_blocks, sensitivity, residual_bus, unit_rhs, start_state, active_set, unit_bus
):
    in_planes = lax.axis_size("bus") == 8 and lax.axis_size("period") > 2
    storage, costate, update = (plane_body if in_planes else plain_body)(
        gain[0],
        schur[0],
        inverse_blocks[0],
        sensitivity,
        residual_bus[0],
        unit_rhs[0],
        start_state,
        active_set[0][:, None],
        unit_bus[None, :],
    )
    return storage[None], costate[None], update[None]


def solution(mesh):
    by_period = P("period", "bus", None)
    placed = (
        by_period,
        by_period,
        by_period,
        P("bus", None),
        by_period,
        by_period,
        P("bus", None),
        P("period", "bus"),
        P(),
    )
    return jax.shard_map(
        body,
        mesh=mesh,
        in_specs=placed,
        out_specs=(by_period, by_period, by_period),
        check_vma=False,
    )
```

```python
import functools

import jax
import jax.numpy as jnp
from jax import lax
from jax.experimental import pallas as pl
from jax.experimental.pallas import tpu as pltpu
from jax.sharding import PartitionSpec as P

BOTH = ("period", "bus")
F32 = jnp.float32
BF16 = jnp.bfloat16
MIB = 1 << 20


def bus_send(block, flip, periods):
    size = lax.axis_size("bus")
    route = [(p * size + b, p * size + (b ^ flip)) for p in periods for b in range(size)]
    return lax.ppermute(block, BOTH, route)


def period_send(block, source, target, flip=0):
    size = lax.axis_size("bus")
    route = [(source * size + b, target * size + (b ^ flip)) for b in range(size)]
    return lax.ppermute(block, BOTH, route)


def times(left, right):
    return jnp.dot(left, right, preferred_element_type=F32)


def times_t(left, right):
    return lax.dot_general(left, right, (((1,), (1,)), ((), ())), preferred_element_type=F32)


def together(*values):
    return lax.optimization_barrier(values)


def line_send(block, pairs, periods):
    size = lax.axis_size("bus")
    route = [
        (p * size + 2 * source + y, p * size + 2 * target + y)
        for p in periods
        for source, target in pairs
        for y in range(2)
    ]
    return lax.ppermute(block, BOTH, route)


def across(block, periods):
    return line_send(block, ((1, 2), (2, 1)), periods)


def outwards(block, periods):
    return line_send(block, ((1, 0), (2, 3)), periods)


def swap_z(pieces, periods):
    return [pieces[0]] + [bus_send(pieces[flip // 2], flip, periods) for flip in (2, 4, 6)]


def in_vmem():
    return pl.BlockSpec(memory_space=pltpu.VMEM)


def anywhere():
    return pl.BlockSpec(memory_space=pl.ANY)


def in_smem():
    return pl.BlockSpec(memory_space=pltpu.SMEM)


def kernel_call(kernel, out_shape, in_specs, scratch, flops, bytes_accessed, mib, out_specs=None):
    return pl.pallas_call(
        kernel,
        out_shape=out_shape,
        in_specs=in_specs,
        out_specs=out_specs or jax.tree.map(lambda _: in_vmem(), out_shape),
        scratch_shapes=scratch,
        compiler_params=pltpu.CompilerParams(vmem_limit_bytes=mib * MIB),
        cost_estimate=pl.CostEstimate(
            flops=flops, bytes_accessed=bytes_accessed, transcendentals=0
        ),
    )


def at(index, size):
    return pl.ds(pl.multiple_of(index * size, size), size)


def front_kernel(
    rank_ref, active, rhs, residual_hbm, inverse_hbm, sens_hbm,
    k0, k2, k4, k6, send, solved,
    residual, inverse, sens, net, solve_t, partial, sems,
):
    rank = rank_ref[0]
    z, y = rank // 2, rank % 2
    loads = [
        pltpu.make_async_copy(residual_hbm, residual, sems.at[0]),
        pltpu.make_async_copy(inverse_hbm, inverse, sems.at[1]),
        pltpu.make_async_copy(sens_hbm, sens, sems.at[2]),
    ]
    for load in loads:
        load.start()
    loads[0].wait()
    net[...] = (residual[...] * (1.0 + 3.0 * active[...].astype(F32))).astype(BF16)
    loads[1].wait()
    blocks = inverse.shape[0] // 256

    @pl.loop(0, blocks)
    def _(i):
        rows = pl.ds(pl.multiple_of(i * 256, 256), 256)
        product = times(inverse[rows, :], net[...])
        solved[rows, :] = product
        solve_t[:, rows] = product.T.astype(BF16)

    loads[2].wait()

    @pl.loop(0, sens.shape[1] // 256)
    def _(i):
        columns = pl.ds(pl.multiple_of(i * 256, 256), 256)
        partial[:, columns] = times(solve_t[...], sens[:, columns])

    units = rhs.shape[0]
    partial[:, at(rank, units)] += rhs[...].T
    rows = k0.shape[0]
    for turn, out in enumerate((k0, k2, k4, k6)):
        here = at(z ^ turn, rows)
        for block in range(4):
            lanes = pl.ds(block * units, units)
            out[:, lanes] = partial[here, at(2 * block + y, units)]
            send[turn, :, lanes] = partial[here, at(2 * block + 1 - y, units)].astype(BF16)


def front(rank, active, rhs, residual, inverse, sens):
    buses, columns = residual.shape
    units = sens.shape[1]
    keep = jax.ShapeDtypeStruct((columns // 4, units // 2), F32)
    send = jax.ShapeDtypeStruct((4, columns // 4, units // 2), BF16)
    return kernel_call(
        front_kernel,
        [keep] * 4 + [send, jax.ShapeDtypeStruct((buses, columns), F32)],
        [in_smem(), in_vmem(), in_vmem(), anywhere(), anywhere(), anywhere()],
        [
            pltpu.VMEM((buses, columns), F32),
            pltpu.VMEM((buses, buses), BF16),
            pltpu.VMEM((buses, units), BF16),
            pltpu.VMEM((buses, columns), BF16),
            pltpu.VMEM((columns, buses), BF16),
            pltpu.VMEM((columns, units), F32),
            pltpu.SemaphoreType.DMA((3,)),
        ],
        2 * buses * columns * (buses + units),
        24 * MIB,
        48,
    )(rank, active, rhs, residual, inverse, sens)


def start_kernel(rank_ref, state, p0, p2, p4, p6):
    for turn, out in enumerate((p0, p2, p4, p6)):
        out[...] = state[:, at((rank_ref[0] // 2) ^ turn, out.shape[1])].astype(BF16)


def start_pieces(rank, state):
    units, columns = state.shape
    return kernel_call(
        start_kernel,
        [jax.ShapeDtypeStruct((units, columns // 4), BF16)] * 4,
        [in_smem(), in_vmem()],
        [],
        state.size,
        6 * state.size,
        8,
    )(rank, state)


def join_kernel(rank_ref, p0, p2, p4, p6, out):
    for turn, piece in enumerate((p0, p2, p4, p6)):
        out[at((rank_ref[0] // 2) ^ turn, piece.shape[0]), :] = piece[...]


def join(rank, pieces):
    units, rights = pieces[0].shape
    return kernel_call(
        join_kernel,
        jax.ShapeDtypeStruct((4 * units, rights), BF16),
        [in_smem()] + [in_vmem()] * 4,
        [],
        units * rights,
        16 * units * rights,
        8,
    )(rank, *pieces)


def pack_kernel(*refs):
    parts, (out, sems) = refs[:3], refs[3:]
    loads = [pltpu.make_async_copy(part, out.at[j], sems.at[j]) for j, part in enumerate(parts)]
    for load in loads:
        load.start()
    for load in loads:
        load.wait()


def pack(parts):
    return kernel_call(
        pack_kernel,
        jax.ShapeDtypeStruct((3, *parts[0].shape), BF16),
        [anywhere()] * 3,
        [pltpu.SemaphoreType.DMA((3,))],
        0,
        12 * parts[0].size,
        48,
    )(*parts)


def backward_kernel(places, turn, own, other, base, former_sums, former_cross, packed, fourth, sums, cross, total):
    units = fourth.shape[0]
    y = places[4]

    def step():
        vector = (own[...].astype(F32) + other[...].astype(F32)).astype(BF16)
        cross_like = jnp.zeros(total.shape, F32)
        total[...] = cross_like
        whole = packed.shape[2]
        for width in range(0, whole, 1024):
            lanes = pl.ds(width, 1024)
            product = None
            for place in range(4):
                weight = packed[place, :, lanes] if place < 3 else fourth[:, lanes]
                blocks = [
                    vector[:, z * units : (z + 1) * units] for z in range(4)
                ]
                chosen = blocks[0]
                for z in range(1, 4):
                    chosen = jnp.where(places[place] == z, blocks[z], chosen)
                term = times(chosen, weight)
                product = term if product is None else product + term
            total[:, lanes] = product
        for block in range(4):
            lanes = pl.ds(block * units, units)
            sums[:, lanes] = (base[:, lanes] + total[:, at(2 * block + y, units)]).astype(BF16)
            cross[:, lanes] = total[:, at(2 * block + 1 - y, units)].astype(BF16)

    def skip():
        sums[...] = former_sums[...]
        cross[...] = former_cross[...]

    pl.when(turn[0] == 1)(step)
    pl.when(turn[0] == 0)(skip)


def backward(places, turn, vector, base, former, weights):
    rows, half = base.shape
    out = jax.ShapeDtypeStruct((rows, half), BF16)
    return kernel_call(
        backward_kernel,
        [out, out],
        [in_smem()] * 2 + [in_vmem()] * 7,
        [pltpu.VMEM((rows, 2 * half), F32)],
        4 * rows * half * half,
        4 * half * half,
        12,
    )(places, turn.astype(jnp.int32).reshape(1), *vector, base, *former, *weights)


def forward_kernel(places, own, other, packed, fourth, *refs):
    subtracted, (out, state) = (refs[0], refs[1:]) if len(refs) > 2 else (None, refs)
    units = fourth.shape[0]
    y = places[4]
    for block in range(4):
        here = pl.ds(block * units, units)
        state[at(2 * block + y, units), :] = own[here, :]
        state[at(2 * block + 1 - y, units), :] = other[here, :]
    for place in range(4):
        weight = packed[place] if place < 3 else fourth[...]
        here = at(places[place], units)
        product = times(weight, state[...])
        if subtracted is not None:
            product = product - subtracted[here, :].astype(F32)
        out[here, :] = product.astype(out.dtype)


def forward(places, state, weights, subtracted=None):
    half, rights = state[0].shape
    extra = () if subtracted is None else (subtracted,)
    return kernel_call(
        forward_kernel,
        jax.ShapeDtypeStruct((half, rights), BF16 if extra else F32),
        [in_smem()] + [in_vmem()] * (4 + len(extra)),
        [pltpu.VMEM((2 * half, rights), BF16)],
        4 * rights * half * half,
        4 * half * half,
        12,
    )(places, *state, *weights, *extra)


def couple_kernel(rank_ref, schur, schur_y, c0, c2, c4, c6, product, cross, costate, whole, mine):
    z, y = rank_ref[0] // 2, rank_ref[0] % 2
    rows, units = c0.shape[0], schur.shape[0]
    for turn, part in enumerate((c0, c2, c4, c6)):
        whole[at(z ^ turn, rows), :] = part[...]
    for block in range(4):
        mine[:, pl.ds(block * units, units)] = schur[:, at(2 * block + y, units)]
    product[...] = times_t(whole[...], mine[...])
    cross[...] = times_t(whole[...], schur_y[...]).astype(BF16)
    costate[...] = whole[:, at(z, units)].astype(F32).T


def couple(rank, schur, schur_y, parts):
    units, half = schur_y.shape
    rows = parts[0].shape[0]
    return kernel_call(
        couple_kernel,
        [
            jax.ShapeDtypeStruct((4 * rows, units), F32),
            jax.ShapeDtypeStruct((4 * rows, units), BF16),
            jax.ShapeDtypeStruct((units, 4 * rows), F32),
        ],
        [in_smem()] + [in_vmem()] * 6,
        [pltpu.VMEM((4 * rows, half), BF16), pltpu.VMEM((units, half), BF16)],
        16 * rows * half * units,
        4 * MIB,
        16,
    )(rank, schur, schur_y, *parts)


def schur_kernel(rank_ref, schur, out):
    units = schur.shape[0]
    for block in range(4):
        out[:, pl.ds(block * units, units)] = schur[:, at(2 * block + 1 - rank_ref[0] % 2, units)]


def schur_cross(rank, schur):
    units, whole = schur.shape
    return kernel_call(
        schur_kernel,
        jax.ShapeDtypeStruct((units, whole // 2), BF16),
        [in_smem(), in_vmem()],
        [],
        units * whole,
        3 * units * whole,
        8,
    )(rank, schur)


def settle_kernel(rank_ref, product, cross, p0, p2, p4, p6, coupling):
    coupling[...] = (product[...] + cross[...].astype(F32)).T
    for turn, out in enumerate((p0, p2, p4, p6)):
        out[...] = coupling[:, at((rank_ref[0] // 2) ^ turn, out.shape[1])].astype(BF16)


def settle(rank, product, cross):
    columns, units = product.shape
    piece = jax.ShapeDtypeStruct((units, columns // 4), BF16)
    return kernel_call(
        settle_kernel,
        [piece] * 4 + [jax.ShapeDtypeStruct((units, columns), F32)],
        [in_smem()] + [in_vmem()] * 2,
        [],
        product.size,
        12 * product.size,
        8,
    )(rank, product, cross)


def finish_kernel(rank_ref, driven, p0, p2, p4, p6, out, terms):
    for turn, piece in enumerate((p0, p2, p4, p6)):
        here = at((rank_ref[0] // 2) ^ turn, piece.shape[0])
        out[here, :] = (driven[here, :] - piece[...].astype(F32)).astype(out.dtype)
        terms[here, :] = piece[...]


def finish(rank, driven, pieces):
    out = jax.ShapeDtypeStruct(driven.shape, BF16)
    return kernel_call(
        finish_kernel,
        [out, out],
        [in_smem()] + [in_vmem()] * 5,
        [],
        driven.size,
        10 * driven.size,
        8,
    )(rank, driven, *pieces)


def picked_kernel(rank_ref, unit_bus, inverse, out):
    buses = inverse.shape[0]
    ids = rank_ref[0] * buses + lax.broadcasted_iota(jnp.int32, (buses, 1), 0)

    @pl.loop(0, out.shape[1] // 256)
    def _(i):
        lanes = at(i, 256)
        placed = (unit_bus[:, lanes] == ids).astype(BF16)
        out[:, lanes] = times(inverse[...], placed).astype(BF16)


def picked(rank, unit_bus, inverse):
    buses, whole = inverse.shape[0], unit_bus.shape[1]
    return kernel_call(
        picked_kernel,
        jax.ShapeDtypeStruct((buses, whole), BF16),
        [in_smem(), in_vmem(), in_vmem()],
        [],
        2 * buses * buses * whole,
        12 * MIB,
        24,
    )(rank, unit_bus, inverse)


def final_kernel(
    rank_ref, coupling, gain, solved_hbm, columns_hbm,
    own, other, near, own4, other4, own6, other6,
    storage, update, solved, columns, whole, sems,
):
    rank = rank_ref[0]
    z, y = rank // 2, rank % 2
    blocks = columns.shape[0] // 256
    sources = ((columns_hbm, columns), (solved_hbm, solved))

    def transfer(i, kind):
        here = at(i, 256)
        if kind == 2:
            return pltpu.make_async_copy(solved.at[here], update.at[here], sems.at[2, i])
        source, target = sources[kind]
        return pltpu.make_async_copy(source.at[here], target.at[here], sems.at[kind, i])

    @pl.loop(0, blocks)
    def _(i):
        for kind in range(2):
            transfer(i, kind).start()

    rights, units = own.shape[1], gain.shape[0]

    def put(turn, halves):
        for block in range(4):
            lanes = slice(block * units, (block + 1) * units)
            for place, half in enumerate(halves):
                which = y if place == 0 else 1 - y
                whole[at(2 * block + which, units), at(z ^ turn, rights)] = half[lanes, :]

    put(0, (own[...], other[...]))
    put(1, (near[0], near[1]))
    put(2, (own4[...], other4[...]))
    put(3, (own6[...], other6[...]))
    storage[...] = times(gain[...], whole[...]) - coupling[...]

    @pl.loop(0, blocks)
    def _(i):
        here = at(i, 256)
        for kind in range(2):
            transfer(i, kind).wait()
        solved[here, :] = solved[here, :] - times(columns[here, :], whole[...])
        transfer(i, 2).start()

    @pl.loop(0, blocks)
    def _(i):
        transfer(i, 2).wait()


def final(rank, coupling, gain, solved, columns, parts):
    buses, rights = solved.shape
    units, whole = gain.shape
    return kernel_call(
        final_kernel,
        [
            jax.ShapeDtypeStruct((units, rights), F32),
            jax.ShapeDtypeStruct((buses, rights), F32),
        ],
        [in_smem()] + [in_vmem()] * 2 + [anywhere()] * 2 + [in_vmem()] * 7,
        [
            pltpu.VMEM((buses, rights), F32),
            pltpu.VMEM((buses, whole), BF16),
            pltpu.VMEM((whole, rights), BF16),
            pltpu.SemaphoreType.DMA((3, buses // 256)),
        ],
        2 * rights * (buses + units) * whole,
        24 * MIB,
        48,
        [in_vmem(), anywhere()],
    )(rank, coupling, gain, solved, columns, *parts)


def plane_body(
    gain, schur, inverse, sens, residual, unit_rhs, start_state, active, unit_bus
):
    period = lax.axis_index("period")
    rank = lax.axis_index("bus").reshape(1)
    last = lax.axis_size("period") - 1
    everyone = tuple(range(last + 1))
    z, y = rank // 2, rank % 2
    far_end = (z == 0) | (z == 3)
    places = jnp.concatenate(
        [z, z ^ 1, jnp.where(far_end, z ^ 2, z ^ 3), jnp.where(far_end, z ^ 3, z ^ 2), y]
    )

    near, middle = bus_send(gain, 2, everyone), across(gain, everyone)
    *keep, send, solved = front(rank, active, unit_rhs, residual, inverse, sens)
    send, start_in = together(send, start_state)
    pieces = swap_z(start_pieces(rank, start_in), everyone)
    near, middle, send, keep, schur_in, pieces = together(
        near, middle, send, keep, schur, pieces
    )
    there = bus_send(send, 1, everyone)
    start = join(rank, pieces)
    middle2, third, there = together(
        across(near, everyone), middle + outwards(middle, everyone), there
    )
    fourth = middle2 + outwards(middle2, everyone)
    schur_y = bus_send(schur_cross(rank, schur_in), 1, everyone)
    unit_right = None
    for turn, flip in ((3, 6), (2, 4), (1, 2), (0, 0)):
        here = keep[turn] + there[turn].astype(F32)
        if flip:
            here = bus_send(here.astype(BF16), flip, everyone).astype(F32)
        unit_right = here if unit_right is None else unit_right + here
    packed, fourth, unit_right, schur_y, columns, start, start_y = together(
        pack([gain, near, third]),
        fourth,
        unit_right,
        schur_y,
        picked(rank, unit_bus, inverse),
        start,
        bus_send(start, 1, everyone),
    )
    weights = [packed, fourth]

    sums, cross = unit_right.astype(BF16), jnp.zeros(unit_right.shape, BF16)
    for target in range(last - 1, -1, -1):
        vector = (
            period_send(sums, target + 1, target),
            cross if target == last - 1 else period_send(cross, target + 1, target, 1),
        )
        sums, cross = backward(places, period == target, vector, unit_right, (sums, cross), weights)
    costate = (sums.astype(F32) + bus_send(cross, 1, everyone).astype(F32)).astype(BF16)
    product, cross, costate_rows = couple(
        rank, schur, schur_y, swap_z([costate] * 4, everyone)
    )
    *pieces, coupling = settle(rank, product, bus_send(cross, 1, everyone))
    driven = forward(places, (start, start_y), weights)
    advanced, coupled = finish(rank, driven, swap_z(pieces, everyone))

    state = (start, start_y)
    for target in range(1, last + 1):
        arrived = (
            period_send(advanced, target - 1, target),
            period_send(advanced, target - 1, target, 1),
        )
        state = tuple(
            jnp.where(period == target, new, old) for new, old in zip(arrived, state, strict=True)
        )
        if target < last:
            advanced = forward(places, arrived, weights, coupled)
    near = bus_send(jnp.stack(state), 2, everyone)
    own4, own6 = bus_send(state[0], 4, everyone), bus_send(state[0], 6, everyone)
    other4, other6 = bus_send(own4, 1, everyone), bus_send(own6, 1, everyone)
    storage, update = final(
        rank, coupling, gain, solved, columns, [*state, near, own4, other4, own6, other6]
    )
    return storage, costate_rows, update


def plain_body(
    gain, schur, inverse, sens, residual, unit_rhs, start_state, active, unit_bus
):
    period = lax.axis_index("period")
    rank = lax.axis_index("bus")
    size = lax.axis_size("bus")
    groups = lax.axis_size("period")
    units, whole = gain.shape
    buses, columns = residual.shape
    rows = columns // size

    def gathered(block):
        return lax.all_gather(block, "bus", axis=0, tiled=True)

    def to_columns(block):
        swapped = lax.all_to_all(block.reshape(size, rows, units), "bus", 0, 0)
        return jnp.transpose(swapped, (1, 0, 2)).reshape(rows, whole)

    weighted = residual * (1.0 + 3.0 * active.astype(F32))
    solve = times(inverse, weighted.astype(BF16)).astype(BF16)
    partial = lax.dot_general(solve, sens, (((0,), (0,)), ((), ())), preferred_element_type=F32)
    place = (0, rank * units)
    own = lax.dynamic_slice(partial, place, (columns, units)) + unit_rhs.T
    partial = lax.dynamic_update_slice(partial, own, place).astype(BF16)
    unit_right = lax.psum_scatter(partial, "bus", scatter_dimension=0, tiled=True).astype(F32)
    gain_whole = gathered(gain)
    costate = unit_right.astype(BF16)
    for target in range(groups - 2, -1, -1):
        later = period_send(costate, target + 1, target)
        current = (unit_right + times(later, gain_whole)).astype(BF16)
        costate = jnp.where(period == target, current, costate)
    costate_whole = gathered(costate)
    coupling = times_t(costate_whole, schur)
    coupled = to_columns(coupling.astype(BF16)).astype(F32)
    state = to_columns(start_state.T.astype(BF16))
    advanced = times_t(state, gain_whole) - coupled
    for target in range(1, groups):
        arrived = period_send(advanced.astype(BF16), target - 1, target)
        state = jnp.where(period == target, arrived, state)
        advanced = times_t(arrived, gain_whole) - coupled
    state_whole = gathered(state)
    storage = times_t(gain, state_whole) - coupling.T
    costate_rows = lax.dynamic_slice_in_dim(costate_whole, rank * units, units, 1).T.astype(F32)
    ids = rank * buses + jnp.arange(buses, dtype=jnp.int32)
    placement = (unit_bus == ids[:, None]).astype(BF16)
    network = (weighted - times_t(placement, state_whole)).astype(BF16)
    return storage, costate_rows, times(inverse, network)


def body(
    gain, schur, inverse_blocks, sensitivity, residual_bus, unit_rhs, start_state, active_set, unit_bus
):
    in_planes = lax.axis_size("bus") == 8 and lax.axis_size("period") > 2
    storage, costate, update = (plane_body if in_planes else plain_body)(
        gain[0],
        schur[0],
        inverse_blocks[0],
        sensitivity,
        residual_bus[0],
        unit_rhs[0],
        start_state,
        active_set[0][:, None],
        unit_bus[None, :],
    )
    return storage[None], costate[None], update[None]


def solution(mesh):
    by_period = P("period", "bus", None)
    placed = (
        by_period,
        by_period,
        by_period,
        P("bus", None),
        by_period,
        by_period,
        P("bus", None),
        P("period", "bus"),
        P(),
    )
    return jax.shard_map(
        body,
        mesh=mesh,
        in_specs=placed,
        out_specs=(by_period, by_period, by_period),
        check_vma=False,
    )
```

```python
import functools

import jax
import jax.numpy as jnp
from jax import lax
from jax.experimental import pallas as pl
from jax.experimental.pallas import tpu as pltpu
from jax.sharding import PartitionSpec as P

BOTH = ("period", "bus")
F32 = jnp.float32
BF16 = jnp.bfloat16
MIB = 1 << 20


def bus_send(block, flip, periods):
    size = lax.axis_size("bus")
    route = [(p * size + b, p * size + (b ^ flip)) for p in periods for b in range(size)]
    return lax.ppermute(block, BOTH, route)


def period_send(block, source, target, flip=0):
    size = lax.axis_size("bus")
    route = [(source * size + b, target * size + (b ^ flip)) for b in range(size)]
    return lax.ppermute(block, BOTH, route)


def times(left, right):
    return jnp.dot(left, right, preferred_element_type=F32)


def times_t(left, right):
    return lax.dot_general(left, right, (((1,), (1,)), ((), ())), preferred_element_type=F32)


def together(*values):
    return lax.optimization_barrier(values)


def line_send(block, pairs, periods):
    size = lax.axis_size("bus")
    route = [
        (p * size + 2 * source + y, p * size + 2 * target + y)
        for p in periods
        for source, target in pairs
        for y in range(2)
    ]
    return lax.ppermute(block, BOTH, route)


def across(block, periods):
    return line_send(block, ((1, 2), (2, 1)), periods)


def outwards(block, periods):
    return line_send(block, ((1, 0), (2, 3)), periods)


def swap_z(pieces, periods):
    return [pieces[0]] + [bus_send(pieces[flip // 2], flip, periods) for flip in (2, 4, 6)]


def in_vmem():
    return pl.BlockSpec(memory_space=pltpu.VMEM)


def anywhere():
    return pl.BlockSpec(memory_space=pl.ANY)


def in_smem():
    return pl.BlockSpec(memory_space=pltpu.SMEM)


def kernel_call(kernel, out_shape, in_specs, scratch, flops, bytes_accessed, mib, out_specs=None):
    return pl.pallas_call(
        kernel,
        out_shape=out_shape,
        in_specs=in_specs,
        out_specs=out_specs or jax.tree.map(lambda _: in_vmem(), out_shape),
        scratch_shapes=scratch,
        compiler_params=pltpu.CompilerParams(vmem_limit_bytes=mib * MIB),
        cost_estimate=pl.CostEstimate(
            flops=flops, bytes_accessed=bytes_accessed, transcendentals=0
        ),
    )


def at(index, size):
    return pl.ds(pl.multiple_of(index * size, size), size)


def front_kernel(
    rank_ref, active, rhs, residual_hbm, inverse_hbm, sens_hbm,
    k0, k2, k4, k6, send, solved,
    residual, inverse, sens, net, solve_t, partial, sems,
):
    rank = rank_ref[0]
    z, y = rank // 2, rank % 2
    loads = [
        pltpu.make_async_copy(residual_hbm, residual, sems.at[0]),
        pltpu.make_async_copy(inverse_hbm, inverse, sems.at[1]),
        pltpu.make_async_copy(sens_hbm, sens, sems.at[2]),
    ]
    for load in loads:
        load.start()
    loads[0].wait()
    net[...] = (residual[...] * (1.0 + 3.0 * active[...].astype(F32))).astype(BF16)
    loads[1].wait()
    blocks = inverse.shape[0] // 256

    @pl.loop(0, blocks)
    def _(i):
        rows = pl.ds(pl.multiple_of(i * 256, 256), 256)
        product = times(inverse[rows, :], net[...])
        solved[rows, :] = product
        solve_t[:, rows] = product.T.astype(BF16)

    loads[2].wait()

    @pl.loop(0, sens.shape[1] // 256)
    def _(i):
        columns = pl.ds(pl.multiple_of(i * 256, 256), 256)
        partial[:, columns] = times(solve_t[...], sens[:, columns])

    units = rhs.shape[0]
    partial[:, at(rank, units)] += rhs[...].T
    rows = k0.shape[0]
    for turn, out in enumerate((k0, k2, k4, k6)):
        here = at(z ^ turn, rows)
        for block in range(4):
            lanes = pl.ds(block * units, units)
            out[:, lanes] = partial[here, at(2 * block + y, units)]
            send[turn, :, lanes] = partial[here, at(2 * block + 1 - y, units)].astype(BF16)


def front(rank, active, rhs, residual, inverse, sens):
    buses, columns = residual.shape
    units = sens.shape[1]
    keep = jax.ShapeDtypeStruct((columns // 4, units // 2), F32)
    send = jax.ShapeDtypeStruct((4, columns // 4, units // 2), BF16)
    return kernel_call(
        front_kernel,
        [keep] * 4 + [send, jax.ShapeDtypeStruct((buses, columns), F32)],
        [in_smem(), in_vmem(), in_vmem(), anywhere(), anywhere(), anywhere()],
        [
            pltpu.VMEM((buses, columns), F32),
            pltpu.VMEM((buses, buses), BF16),
            pltpu.VMEM((buses, units), BF16),
            pltpu.VMEM((buses, columns), BF16),
            pltpu.VMEM((columns, buses), BF16),
            pltpu.VMEM((columns, units), F32),
            pltpu.SemaphoreType.DMA((3,)),
        ],
        2 * buses * columns * (buses + units),
        24 * MIB,
        48,
    )(rank, active, rhs, residual, inverse, sens)


def start_kernel(rank_ref, state, p0, p2, p4, p6):
    for turn, out in enumerate((p0, p2, p4, p6)):
        out[...] = state[:, at((rank_ref[0] // 2) ^ turn, out.shape[1])].astype(BF16)


def start_pieces(rank, state):
    units, columns = state.shape
    return kernel_call(
        start_kernel,
        [jax.ShapeDtypeStruct((units, columns // 4), BF16)] * 4,
        [in_smem(), in_vmem()],
        [],
        state.size,
        6 * state.size,
        8,
    )(rank, state)


def join_kernel(rank_ref, p0, p2, p4, p6, out):
    for turn, piece in enumerate((p0, p2, p4, p6)):
        out[at((rank_ref[0] // 2) ^ turn, piece.shape[0]), :] = piece[...]


def join(rank, pieces):
    units, rights = pieces[0].shape
    return kernel_call(
        join_kernel,
        jax.ShapeDtypeStruct((4 * units, rights), BF16),
        [in_smem()] + [in_vmem()] * 4,
        [],
        units * rights,
        16 * units * rights,
        8,
    )(rank, *pieces)


def pack_kernel(*refs):
    parts, (out, sems) = refs[:3], refs[3:]
    loads = [pltpu.make_async_copy(part, out.at[j], sems.at[j]) for j, part in enumerate(parts)]
    for load in loads:
        load.start()
    for load in loads:
        load.wait()


def pack(parts):
    return kernel_call(
        pack_kernel,
        jax.ShapeDtypeStruct((3, *parts[0].shape), BF16),
        [anywhere()] * 3,
        [pltpu.SemaphoreType.DMA((3,))],
        0,
        12 * parts[0].size,
        8,
    )(*parts)


def backward_kernel(places, turn, own, other, base, former_sums, former_cross, packed, fourth, sums, cross, total):
    units = fourth.shape[0]
    y = places[4]

    def step():
        vector = (own[...].astype(F32) + other[...].astype(F32)).astype(BF16)
        cross_like = jnp.zeros(total.shape, F32)
        total[...] = cross_like
        whole = packed.shape[2]
        for width in range(0, whole, 1024):
            lanes = pl.ds(width, 1024)
            product = None
            for place in range(4):
                weight = packed[place, :, lanes] if place < 3 else fourth[:, lanes]
                blocks = [
                    vector[:, z * units : (z + 1) * units] for z in range(4)
                ]
                chosen = blocks[0]
                for z in range(1, 4):
                    chosen = jnp.where(places[place] == z, blocks[z], chosen)
                term = times(chosen, weight)
                product = term if product is None else product + term
            total[:, lanes] = product
        for block in range(4):
            lanes = pl.ds(block * units, units)
            sums[:, lanes] = (base[:, lanes] + total[:, at(2 * block + y, units)]).astype(BF16)
            cross[:, lanes] = total[:, at(2 * block + 1 - y, units)].astype(BF16)

    def skip():
        sums[...] = former_sums[...]
        cross[...] = former_cross[...]

    pl.when(turn[0] == 1)(step)
    pl.when(turn[0] == 0)(skip)


def backward(places, turn, vector, base, former, weights):
    rows, half = base.shape
    out = jax.ShapeDtypeStruct((rows, half), BF16)
    return kernel_call(
        backward_kernel,
        [out, out],
        [in_smem()] * 2 + [in_vmem()] * 7,
        [pltpu.VMEM((rows, 2 * half), F32)],
        4 * rows * half * half,
        4 * half * half,
        12,
    )(places, turn.astype(jnp.int32).reshape(1), *vector, base, *former, *weights)


def forward_kernel(places, own, other, packed, fourth, *refs):
    subtracted, (out, state) = (refs[0], refs[1:]) if len(refs) > 2 else (None, refs)
    units = fourth.shape[0]
    y = places[4]
    for block in range(4):
        here = pl.ds(block * units, units)
        state[at(2 * block + y, units), :] = own[here, :]
        state[at(2 * block + 1 - y, units), :] = other[here, :]
    for place in range(4):
        weight = packed[place] if place < 3 else fourth[...]
        here = at(places[place], units)
        product = times(weight, state[...])
        if subtracted is not None:
            product = product - subtracted[here, :].astype(F32)
        out[here, :] = product.astype(out.dtype)


def forward(places, state, weights, subtracted=None):
    half, rights = state[0].shape
    extra = () if subtracted is None else (subtracted,)
    return kernel_call(
        forward_kernel,
        jax.ShapeDtypeStruct((half, rights), BF16 if extra else F32),
        [in_smem()] + [in_vmem()] * (4 + len(extra)),
        [pltpu.VMEM((2 * half, rights), BF16)],
        4 * rights * half * half,
        4 * half * half,
        12,
    )(places, *state, *weights, *extra)


def couple_kernel(rank_ref, schur, schur_y, c0, c2, c4, c6, product, cross, costate, whole, mine):
    z, y = rank_ref[0] // 2, rank_ref[0] % 2
    rows, units = c0.shape[0], schur.shape[0]
    for turn, part in enumerate((c0, c2, c4, c6)):
        whole[at(z ^ turn, rows), :] = part[...]
    for block in range(4):
        mine[:, pl.ds(block * units, units)] = schur[:, at(2 * block + y, units)]
    product[...] = times_t(whole[...], mine[...])
    cross[...] = times_t(whole[...], schur_y[...]).astype(BF16)
    costate[...] = whole[:, at(z, units)].astype(F32).T


def couple(rank, schur, schur_y, parts):
    units, half = schur_y.shape
    rows = parts[0].shape[0]
    return kernel_call(
        couple_kernel,
        [
            jax.ShapeDtypeStruct((4 * rows, units), F32),
            jax.ShapeDtypeStruct((4 * rows, units), BF16),
            jax.ShapeDtypeStruct((units, 4 * rows), F32),
        ],
        [in_smem()] + [in_vmem()] * 6,
        [pltpu.VMEM((4 * rows, half), BF16), pltpu.VMEM((units, half), BF16)],
        16 * rows * half * units,
        4 * MIB,
        16,
    )(rank, schur, schur_y, *parts)


def schur_kernel(rank_ref, schur, out):
    units = schur.shape[0]
    for block in range(4):
        out[:, pl.ds(block * units, units)] = schur[:, at(2 * block + 1 - rank_ref[0] % 2, units)]


def schur_cross(rank, schur):
    units, whole = schur.shape
    return kernel_call(
        schur_kernel,
        jax.ShapeDtypeStruct((units, whole // 2), BF16),
        [in_smem(), in_vmem()],
        [],
        units * whole,
        3 * units * whole,
        8,
    )(rank, schur)


def settle_kernel(rank_ref, product, cross, p0, p2, p4, p6, coupling):
    coupling[...] = (product[...] + cross[...].astype(F32)).T
    for turn, out in enumerate((p0, p2, p4, p6)):
        out[...] = coupling[:, at((rank_ref[0] // 2) ^ turn, out.shape[1])].astype(BF16)


def settle(rank, product, cross):
    columns, units = product.shape
    piece = jax.ShapeDtypeStruct((units, columns // 4), BF16)
    return kernel_call(
        settle_kernel,
        [piece] * 4 + [jax.ShapeDtypeStruct((units, columns), F32)],
        [in_smem()] + [in_vmem()] * 2,
        [],
        product.size,
        12 * product.size,
        8,
    )(rank, product, cross)


def finish_kernel(rank_ref, driven, p0, p2, p4, p6, out, terms):
    for turn, piece in enumerate((p0, p2, p4, p6)):
        here = at((rank_ref[0] // 2) ^ turn, piece.shape[0])
        out[here, :] = (driven[here, :] - piece[...].astype(F32)).astype(out.dtype)
        terms[here, :] = piece[...]


def finish(rank, driven, pieces):
    out = jax.ShapeDtypeStruct(driven.shape, BF16)
    return kernel_call(
        finish_kernel,
        [out, out],
        [in_smem()] + [in_vmem()] * 5,
        [],
        driven.size,
        10 * driven.size,
        8,
    )(rank, driven, *pieces)


def picked_kernel(rank_ref, unit_bus, inverse, out):
    buses = inverse.shape[0]
    ids = rank_ref[0] * buses + lax.broadcasted_iota(jnp.int32, (buses, 1), 0)

    @pl.loop(0, out.shape[1] // 256)
    def _(i):
        lanes = at(i, 256)
        placed = (unit_bus[:, lanes] == ids).astype(BF16)
        out[:, lanes] = times(inverse[...], placed).astype(BF16)


def picked(rank, unit_bus, inverse):
    buses, whole = inverse.shape[0], unit_bus.shape[1]
    return kernel_call(
        picked_kernel,
        jax.ShapeDtypeStruct((buses, whole), BF16),
        [in_smem(), in_vmem(), in_vmem()],
        [],
        2 * buses * buses * whole,
        12 * MIB,
        24,
    )(rank, unit_bus, inverse)


def final_kernel(
    rank_ref, coupling, gain, solved_hbm, columns_hbm,
    own, other, near, own4, other4, own6, other6,
    storage, update, solved, columns, whole, sems,
):
    rank = rank_ref[0]
    z, y = rank // 2, rank % 2
    blocks = columns.shape[0] // 256
    sources = ((columns_hbm, columns), (solved_hbm, solved))

    def transfer(i, kind):
        here = at(i, 256)
        if kind == 2:
            return pltpu.make_async_copy(solved.at[here], update.at[here], sems.at[2, i])
        source, target = sources[kind]
        return pltpu.make_async_copy(source.at[here], target.at[here], sems.at[kind, i])

    @pl.loop(0, blocks)
    def _(i):
        for kind in range(2):
            transfer(i, kind).start()

    rights, units = own.shape[1], gain.shape[0]

    def put(turn, halves):
        for block in range(4):
            lanes = slice(block * units, (block + 1) * units)
            for place, half in enumerate(halves):
                which = y if place == 0 else 1 - y
                whole[at(2 * block + which, units), at(z ^ turn, rights)] = half[lanes, :]

    put(0, (own[...], other[...]))
    put(1, (near[0], near[1]))
    put(2, (own4[...], other4[...]))
    put(3, (own6[...], other6[...]))
    storage[...] = times(gain[...], whole[...]) - coupling[...]

    @pl.loop(0, blocks)
    def _(i):
        here = at(i, 256)
        for kind in range(2):
            transfer(i, kind).wait()
        solved[here, :] = solved[here, :] - times(columns[here, :], whole[...])
        transfer(i, 2).start()

    @pl.loop(0, blocks)
    def _(i):
        transfer(i, 2).wait()


def final(rank, coupling, gain, solved, columns, parts):
    buses, rights = solved.shape
    units, whole = gain.shape
    return kernel_call(
        final_kernel,
        [
            jax.ShapeDtypeStruct((units, rights), F32),
            jax.ShapeDtypeStruct((buses, rights), F32),
        ],
        [in_smem()] + [in_vmem()] * 2 + [anywhere()] * 2 + [in_vmem()] * 7,
        [
            pltpu.VMEM((buses, rights), F32),
            pltpu.VMEM((buses, whole), BF16),
            pltpu.VMEM((whole, rights), BF16),
            pltpu.SemaphoreType.DMA((3, buses // 256)),
        ],
        2 * rights * (buses + units) * whole,
        24 * MIB,
        48,
        [in_vmem(), anywhere()],
    )(rank, coupling, gain, solved, columns, *parts)


def plane_body(
    gain, schur, inverse, sens, residual, unit_rhs, start_state, active, unit_bus
):
    period = lax.axis_index("period")
    rank = lax.axis_index("bus").reshape(1)
    last = lax.axis_size("period") - 1
    everyone = tuple(range(last + 1))
    z, y = rank // 2, rank % 2
    far_end = (z == 0) | (z == 3)
    places = jnp.concatenate(
        [z, z ^ 1, jnp.where(far_end, z ^ 2, z ^ 3), jnp.where(far_end, z ^ 3, z ^ 2), y]
    )

    near, middle = bus_send(gain, 2, everyone), across(gain, everyone)
    *keep, send, solved = front(rank, active, unit_rhs, residual, inverse, sens)
    send, start_in = together(send, start_state)
    pieces = swap_z(start_pieces(rank, start_in), everyone)
    near, middle, send, keep, schur_in, pieces = together(
        near, middle, send, keep, schur, pieces
    )
    there = bus_send(send, 1, everyone)
    start = join(rank, pieces)
    middle2, third, there = together(
        across(near, everyone), middle + outwards(middle, everyone), there
    )
    fourth = middle2 + outwards(middle2, everyone)
    schur_y = bus_send(schur_cross(rank, schur_in), 1, everyone)
    unit_right = None
    for turn, flip in ((3, 6), (2, 4), (1, 2), (0, 0)):
        here = keep[turn] + there[turn].astype(F32)
        if flip:
            here = bus_send(here.astype(BF16), flip, everyone).astype(F32)
        unit_right = here if unit_right is None else unit_right + here
    gain, near, third, fourth, unit_right, schur_y, columns, start, start_y = together(
        gain,
        near,
        third,
        fourth,
        unit_right,
        schur_y,
        picked(rank, unit_bus, inverse),
        start,
        bus_send(start, 1, everyone),
    )

    sums, cross = unit_right.astype(BF16), jnp.zeros(unit_right.shape, BF16)
    for target in range(last - 1, -1, -1):
        vector = (
            period_send(sums, target + 1, target),
            cross if target == last - 1 else period_send(cross, target + 1, target, 1),
        )
        gain, near, third, fourth, sums, cross = together(gain, near, third, fourth, sums, cross)
        weights = [pack([gain, near, third]), fourth]
        sums, cross = backward(places, period == target, vector, unit_right, (sums, cross), weights)
    costate = (sums.astype(F32) + bus_send(cross, 1, everyone).astype(F32)).astype(BF16)
    product, cross, costate_rows = couple(
        rank, schur, schur_y, swap_z([costate] * 4, everyone)
    )
    *pieces, coupling = settle(rank, product, bus_send(cross, 1, everyone))
    driven = forward(places, (start, start_y), weights)
    advanced, coupled = finish(rank, driven, swap_z(pieces, everyone))

    state = (start, start_y)
    for target in range(1, last + 1):
        arrived = (
            period_send(advanced, target - 1, target),
            period_send(advanced, target - 1, target, 1),
        )
        state = tuple(
            jnp.where(period == target, new, old) for new, old in zip(arrived, state, strict=True)
        )
        if target < last:
            advanced = forward(places, arrived, weights, coupled)
    near = bus_send(jnp.stack(state), 2, everyone)
    own4, own6 = bus_send(state[0], 4, everyone), bus_send(state[0], 6, everyone)
    other4, other6 = bus_send(own4, 1, everyone), bus_send(own6, 1, everyone)
    storage, update = final(
        rank, coupling, gain, solved, columns, [*state, near, own4, other4, own6, other6]
    )
    return storage, costate_rows, update


def plain_body(
    gain, schur, inverse, sens, residual, unit_rhs, start_state, active, unit_bus
):
    period = lax.axis_index("period")
    rank = lax.axis_index("bus")
    size = lax.axis_size("bus")
    groups = lax.axis_size("period")
    units, whole = gain.shape
    buses, columns = residual.shape
    rows = columns // size

    def gathered(block):
        return lax.all_gather(block, "bus", axis=0, tiled=True)

    def to_columns(block):
        swapped = lax.all_to_all(block.reshape(size, rows, units), "bus", 0, 0)
        return jnp.transpose(swapped, (1, 0, 2)).reshape(rows, whole)

    weighted = residual * (1.0 + 3.0 * active.astype(F32))
    solve = times(inverse, weighted.astype(BF16)).astype(BF16)
    partial = lax.dot_general(solve, sens, (((0,), (0,)), ((), ())), preferred_element_type=F32)
    place = (0, rank * units)
    own = lax.dynamic_slice(partial, place, (columns, units)) + unit_rhs.T
    partial = lax.dynamic_update_slice(partial, own, place).astype(BF16)
    unit_right = lax.psum_scatter(partial, "bus", scatter_dimension=0, tiled=True).astype(F32)
    gain_whole = gathered(gain)
    costate = unit_right.astype(BF16)
    for target in range(groups - 2, -1, -1):
        later = period_send(costate, target + 1, target)
        current = (unit_right + times(later, gain_whole)).astype(BF16)
        costate = jnp.where(period == target, current, costate)
    costate_whole = gathered(costate)
    coupling = times_t(costate_whole, schur)
    coupled = to_columns(coupling.astype(BF16)).astype(F32)
    state = to_columns(start_state.T.astype(BF16))
    advanced = times_t(state, gain_whole) - coupled
    for target in range(1, groups):
        arrived = period_send(advanced.astype(BF16), target - 1, target)
        state = jnp.where(period == target, arrived, state)
        advanced = times_t(arrived, gain_whole) - coupled
    state_whole = gathered(state)
    storage = times_t(gain, state_whole) - coupling.T
    costate_rows = lax.dynamic_slice_in_dim(costate_whole, rank * units, units, 1).T.astype(F32)
    ids = rank * buses + jnp.arange(buses, dtype=jnp.int32)
    placement = (unit_bus == ids[:, None]).astype(BF16)
    network = (weighted - times_t(placement, state_whole)).astype(BF16)
    return storage, costate_rows, times(inverse, network)


def body(
    gain, schur, inverse_blocks, sensitivity, residual_bus, unit_rhs, start_state, active_set, unit_bus
):
    in_planes = lax.axis_size("bus") == 8 and lax.axis_size("period") > 2
    storage, costate, update = (plane_body if in_planes else plain_body)(
        gain[0],
        schur[0],
        inverse_blocks[0],
        sensitivity,
        residual_bus[0],
        unit_rhs[0],
        start_state,
        active_set[0][:, None],
        unit_bus[None, :],
    )
    return storage[None], costate[None], update[None]


def solution(mesh):
    by_period = P("period", "bus", None)
    placed = (
        by_period,
        by_period,
        by_period,
        P("bus", None),
        by_period,
        by_period,
        P("bus", None),
        P("period", "bus"),
        P(),
    )
    return jax.shard_map(
        body,
        mesh=mesh,
        in_specs=placed,
        out_specs=(by_period, by_period, by_period),
        check_vma=False,
    )
```

```python
import functools

import jax
import jax.numpy as jnp
from jax import lax
from jax.experimental import pallas as pl
from jax.experimental.pallas import tpu as pltpu
from jax.sharding import PartitionSpec as P

BOTH = ("period", "bus")
F32 = jnp.float32
BF16 = jnp.bfloat16
MIB = 1 << 20


def bus_send(block, flip, periods):
    size = lax.axis_size("bus")
    route = [(p * size + b, p * size + (b ^ flip)) for p in periods for b in range(size)]
    return lax.ppermute(block, BOTH, route)


def period_send(block, source, target, flip=0):
    size = lax.axis_size("bus")
    route = [(source * size + b, target * size + (b ^ flip)) for b in range(size)]
    return lax.ppermute(block, BOTH, route)


def times(left, right):
    return jnp.dot(left, right, preferred_element_type=F32)


def times_t(left, right):
    return lax.dot_general(left, right, (((1,), (1,)), ((), ())), preferred_element_type=F32)


def together(*values):
    return lax.optimization_barrier(values)


def line_send(block, pairs, periods):
    size = lax.axis_size("bus")
    route = [
        (p * size + 2 * source + y, p * size + 2 * target + y)
        for p in periods
        for source, target in pairs
        for y in range(2)
    ]
    return lax.ppermute(block, BOTH, route)


def across(block, periods):
    return line_send(block, ((1, 2), (2, 1)), periods)


def outwards(block, periods):
    return line_send(block, ((1, 0), (2, 3)), periods)


def swap_z(pieces, periods):
    return [pieces[0]] + [bus_send(pieces[flip // 2], flip, periods) for flip in (2, 4, 6)]


def in_vmem():
    return pl.BlockSpec(memory_space=pltpu.VMEM)


def anywhere():
    return pl.BlockSpec(memory_space=pl.ANY)


def in_smem():
    return pl.BlockSpec(memory_space=pltpu.SMEM)


def kernel_call(kernel, out_shape, in_specs, scratch, flops, bytes_accessed, mib, out_specs=None):
    return pl.pallas_call(
        kernel,
        out_shape=out_shape,
        in_specs=in_specs,
        out_specs=out_specs or jax.tree.map(lambda _: in_vmem(), out_shape),
        scratch_shapes=scratch,
        compiler_params=pltpu.CompilerParams(vmem_limit_bytes=mib * MIB),
        cost_estimate=pl.CostEstimate(
            flops=flops, bytes_accessed=bytes_accessed, transcendentals=0
        ),
    )


def at(index, size):
    return pl.ds(pl.multiple_of(index * size, size), size)


def front_kernel(
    rank_ref, active, rhs, residual_hbm, inverse_hbm, sens_hbm,
    k0, k2, k4, k6, send, solved,
    residual, inverse, sens, net, solve_t, partial, sems,
):
    rank = rank_ref[0]
    z, y = rank // 2, rank % 2
    loads = [
        pltpu.make_async_copy(residual_hbm, residual, sems.at[0]),
        pltpu.make_async_copy(inverse_hbm, inverse, sems.at[1]),
        pltpu.make_async_copy(sens_hbm, sens, sems.at[2]),
    ]
    for load in loads:
        load.start()
    loads[0].wait()
    net[...] = (residual[...] * (1.0 + 3.0 * active[...].astype(F32))).astype(BF16)
    loads[1].wait()
    blocks = inverse.shape[0] // 256

    @pl.loop(0, blocks)
    def _(i):
        rows = pl.ds(pl.multiple_of(i * 256, 256), 256)
        product = times(inverse[rows, :], net[...])
        solved[rows, :] = product
        solve_t[:, rows] = product.T.astype(BF16)

    loads[2].wait()

    @pl.loop(0, sens.shape[1] // 256)
    def _(i):
        columns = pl.ds(pl.multiple_of(i * 256, 256), 256)
        partial[:, columns] = times(solve_t[...], sens[:, columns])

    units = rhs.shape[0]
    partial[:, at(rank, units)] += rhs[...].T
    rows = k0.shape[0]
    for turn, out in enumerate((k0, k2, k4, k6)):
        here = at(z ^ turn, rows)
        for block in range(4):
            lanes = pl.ds(block * units, units)
            out[:, lanes] = partial[here, at(2 * block + y, units)]
            send[turn, :, lanes] = partial[here, at(2 * block + 1 - y, units)].astype(BF16)


def front(rank, active, rhs, residual, inverse, sens):
    buses, columns = residual.shape
    units = sens.shape[1]
    keep = jax.ShapeDtypeStruct((columns // 4, units // 2), F32)
    send = jax.ShapeDtypeStruct((4, columns // 4, units // 2), BF16)
    return kernel_call(
        front_kernel,
        [keep] * 4 + [send, jax.ShapeDtypeStruct((buses, columns), F32)],
        [in_smem(), in_vmem(), in_vmem(), anywhere(), anywhere(), anywhere()],
        [
            pltpu.VMEM((buses, columns), F32),
            pltpu.VMEM((buses, buses), BF16),
            pltpu.VMEM((buses, units), BF16),
            pltpu.VMEM((buses, columns), BF16),
            pltpu.VMEM((columns, buses), BF16),
            pltpu.VMEM((columns, units), F32),
            pltpu.SemaphoreType.DMA((3,)),
        ],
        2 * buses * columns * (buses + units),
        24 * MIB,
        48,
    )(rank, active, rhs, residual, inverse, sens)


def start_kernel(rank_ref, state, p0, p2, p4, p6):
    for turn, out in enumerate((p0, p2, p4, p6)):
        out[...] = state[:, at((rank_ref[0] // 2) ^ turn, out.shape[1])].astype(BF16)


def start_pieces(rank, state):
    units, columns = state.shape
    return kernel_call(
        start_kernel,
        [jax.ShapeDtypeStruct((units, columns // 4), BF16)] * 4,
        [in_smem(), in_vmem()],
        [],
        state.size,
        6 * state.size,
        8,
    )(rank, state)


def join_kernel(rank_ref, p0, p2, p4, p6, out):
    for turn, piece in enumerate((p0, p2, p4, p6)):
        out[at((rank_ref[0] // 2) ^ turn, piece.shape[0]), :] = piece[...]


def join(rank, pieces):
    units, rights = pieces[0].shape
    return kernel_call(
        join_kernel,
        jax.ShapeDtypeStruct((4 * units, rights), BF16),
        [in_smem()] + [in_vmem()] * 4,
        [],
        units * rights,
        16 * units * rights,
        8,
    )(rank, *pieces)


def pack_kernel(*refs):
    parts, (out, sems) = refs[:3], refs[3:]
    loads = [pltpu.make_async_copy(part, out.at[j], sems.at[j]) for j, part in enumerate(parts)]
    for load in loads:
        load.start()
    for load in loads:
        load.wait()


def pack(parts):
    return kernel_call(
        pack_kernel,
        jax.ShapeDtypeStruct((3, *parts[0].shape), BF16),
        [anywhere()] * 3,
        [pltpu.SemaphoreType.DMA((3,))],
        0,
        12 * parts[0].size,
        8,
    )(*parts)


def backward_kernel(places, turn, own, other, base, former_sums, former_cross, packed, fourth, sums, cross, total):
    units = fourth.shape[0]
    y = places[4]

    def step():
        vector = (own[...].astype(F32) + other[...].astype(F32)).astype(BF16)
        cross_like = jnp.zeros(total.shape, F32)
        total[...] = cross_like
        whole = packed.shape[2]
        for width in range(0, whole, 1024):
            lanes = pl.ds(width, 1024)
            product = None
            for place in range(4):
                weight = packed[place, :, lanes] if place < 3 else fourth[:, lanes]
                blocks = [
                    vector[:, z * units : (z + 1) * units] for z in range(4)
                ]
                chosen = blocks[0]
                for z in range(1, 4):
                    chosen = jnp.where(places[place] == z, blocks[z], chosen)
                term = times(chosen, weight)
                product = term if product is None else product + term
            total[:, lanes] = product
        for block in range(4):
            lanes = pl.ds(block * units, units)
            sums[:, lanes] = (base[:, lanes] + total[:, at(2 * block + y, units)]).astype(BF16)
            cross[:, lanes] = total[:, at(2 * block + 1 - y, units)].astype(BF16)

    def skip():
        sums[...] = former_sums[...]
        cross[...] = former_cross[...]

    pl.when(turn[0] == 1)(step)
    pl.when(turn[0] == 0)(skip)


def backward(places, turn, vector, base, former, weights):
    rows, half = base.shape
    out = jax.ShapeDtypeStruct((rows, half), BF16)
    return kernel_call(
        backward_kernel,
        [out, out],
        [in_smem()] * 2 + [in_vmem()] * 7,
        [pltpu.VMEM((rows, 2 * half), F32)],
        4 * rows * half * half,
        4 * half * half,
        12,
    )(places, turn.astype(jnp.int32).reshape(1), *vector, base, *former, *weights)


def forward_kernel(places, own, other, packed, fourth, *refs):
    subtracted, (out, state) = (refs[0], refs[1:]) if len(refs) > 2 else (None, refs)
    units = fourth.shape[0]
    y = places[4]
    for block in range(4):
        here = pl.ds(block * units, units)
        state[at(2 * block + y, units), :] = own[here, :]
        state[at(2 * block + 1 - y, units), :] = other[here, :]
    for place in range(4):
        weight = packed[place] if place < 3 else fourth[...]
        here = at(places[place], units)
        product = times(weight, state[...])
        if subtracted is not None:
            product = product - subtracted[here, :].astype(F32)
        out[here, :] = product.astype(out.dtype)


def forward(places, state, weights, subtracted=None):
    half, rights = state[0].shape
    extra = () if subtracted is None else (subtracted,)
    return kernel_call(
        forward_kernel,
        jax.ShapeDtypeStruct((half, rights), BF16 if extra else F32),
        [in_smem()] + [in_vmem()] * (4 + len(extra)),
        [pltpu.VMEM((2 * half, rights), BF16)],
        4 * rights * half * half,
        4 * half * half,
        12,
    )(places, *state, *weights, *extra)


def couple_kernel(rank_ref, schur, schur_y, c0, c2, c4, c6, product, cross, costate, whole, mine):
    z, y = rank_ref[0] // 2, rank_ref[0] % 2
    rows, units = c0.shape[0], schur.shape[0]
    for turn, part in enumerate((c0, c2, c4, c6)):
        whole[at(z ^ turn, rows), :] = part[...]
    for block in range(4):
        mine[:, pl.ds(block * units, units)] = schur[:, at(2 * block + y, units)]
    product[...] = times_t(whole[...], mine[...])
    cross[...] = times_t(whole[...], schur_y[...]).astype(BF16)
    costate[...] = whole[:, at(z, units)].astype(F32).T


def couple(rank, schur, schur_y, parts):
    units, half = schur_y.shape
    rows = parts[0].shape[0]
    return kernel_call(
        couple_kernel,
        [
            jax.ShapeDtypeStruct((4 * rows, units), F32),
            jax.ShapeDtypeStruct((4 * rows, units), BF16),
            jax.ShapeDtypeStruct((units, 4 * rows), F32),
        ],
        [in_smem()] + [in_vmem()] * 6,
        [pltpu.VMEM((4 * rows, half), BF16), pltpu.VMEM((units, half), BF16)],
        16 * rows * half * units,
        4 * MIB,
        16,
    )(rank, schur, schur_y, *parts)


def schur_kernel(rank_ref, schur, out):
    units = schur.shape[0]
    for block in range(4):
        out[:, pl.ds(block * units, units)] = schur[:, at(2 * block + 1 - rank_ref[0] % 2, units)]


def schur_cross(rank, schur):
    units, whole = schur.shape
    return kernel_call(
        schur_kernel,
        jax.ShapeDtypeStruct((units, whole // 2), BF16),
        [in_smem(), in_vmem()],
        [],
        units * whole,
        3 * units * whole,
        8,
    )(rank, schur)


def settle_kernel(rank_ref, product, cross, p0, p2, p4, p6, coupling):
    coupling[...] = (product[...] + cross[...].astype(F32)).T
    for turn, out in enumerate((p0, p2, p4, p6)):
        out[...] = coupling[:, at((rank_ref[0] // 2) ^ turn, out.shape[1])].astype(BF16)


def settle(rank, product, cross):
    columns, units = product.shape
    piece = jax.ShapeDtypeStruct((units, columns // 4), BF16)
    return kernel_call(
        settle_kernel,
        [piece] * 4 + [jax.ShapeDtypeStruct((units, columns), F32)],
        [in_smem()] + [in_vmem()] * 2,
        [],
        product.size,
        12 * product.size,
        8,
    )(rank, product, cross)


def finish_kernel(rank_ref, driven, p0, p2, p4, p6, out, terms):
    for turn, piece in enumerate((p0, p2, p4, p6)):
        here = at((rank_ref[0] // 2) ^ turn, piece.shape[0])
        out[here, :] = (driven[here, :] - piece[...].astype(F32)).astype(out.dtype)
        terms[here, :] = piece[...]


def finish(rank, driven, pieces):
    out = jax.ShapeDtypeStruct(driven.shape, BF16)
    return kernel_call(
        finish_kernel,
        [out, out],
        [in_smem()] + [in_vmem()] * 5,
        [],
        driven.size,
        10 * driven.size,
        8,
    )(rank, driven, *pieces)


def picked_kernel(rank_ref, unit_bus, inverse, out):
    buses = inverse.shape[0]
    ids = rank_ref[0] * buses + lax.broadcasted_iota(jnp.int32, (buses, 1), 0)

    @pl.loop(0, out.shape[1] // 256)
    def _(i):
        lanes = at(i, 256)
        placed = (unit_bus[:, lanes] == ids).astype(BF16)
        out[:, lanes] = times(inverse[...], placed).astype(BF16)


def picked(rank, unit_bus, inverse):
    buses, whole = inverse.shape[0], unit_bus.shape[1]
    return kernel_call(
        picked_kernel,
        jax.ShapeDtypeStruct((buses, whole), BF16),
        [in_smem(), in_vmem(), in_vmem()],
        [],
        2 * buses * buses * whole,
        12 * MIB,
        24,
    )(rank, unit_bus, inverse)


def final_kernel(
    rank_ref, coupling, gain, solved_hbm, columns_hbm,
    own, other, near, own4, other4, own6, other6,
    storage, update, solved, columns, whole, sems,
):
    rank = rank_ref[0]
    z, y = rank // 2, rank % 2
    blocks = columns.shape[0] // 256
    sources = ((columns_hbm, columns), (solved_hbm, solved))

    def transfer(i, kind):
        here = at(i, 256)
        if kind == 2:
            return pltpu.make_async_copy(solved.at[here], update.at[here], sems.at[2, i])
        source, target = sources[kind]
        return pltpu.make_async_copy(source.at[here], target.at[here], sems.at[kind, i])

    @pl.loop(0, blocks)
    def _(i):
        for kind in range(2):
            transfer(i, kind).start()

    rights, units = own.shape[1], gain.shape[0]

    def put(turn, halves):
        for block in range(4):
            lanes = slice(block * units, (block + 1) * units)
            for place, half in enumerate(halves):
                which = y if place == 0 else 1 - y
                whole[at(2 * block + which, units), at(z ^ turn, rights)] = half[lanes, :]

    put(0, (own[...], other[...]))
    put(1, (near[0], near[1]))
    put(2, (own4[...], other4[...]))
    put(3, (own6[...], other6[...]))
    storage[...] = times(gain[...], whole[...]) - coupling[...]

    @pl.loop(0, blocks)
    def _(i):
        here = at(i, 256)
        for kind in range(2):
            transfer(i, kind).wait()
        solved[here, :] = solved[here, :] - times(columns[here, :], whole[...])
        transfer(i, 2).start()

    @pl.loop(0, blocks)
    def _(i):
        transfer(i, 2).wait()


def final(rank, coupling, gain, solved, columns, parts):
    buses, rights = solved.shape
    units, whole = gain.shape
    return kernel_call(
        final_kernel,
        [
            jax.ShapeDtypeStruct((units, rights), F32),
            jax.ShapeDtypeStruct((buses, rights), F32),
        ],
        [in_smem()] + [in_vmem()] * 2 + [anywhere()] * 2 + [in_vmem()] * 7,
        [
            pltpu.VMEM((buses, rights), F32),
            pltpu.VMEM((buses, whole), BF16),
            pltpu.VMEM((whole, rights), BF16),
            pltpu.SemaphoreType.DMA((3, buses // 256)),
        ],
        2 * rights * (buses + units) * whole,
        24 * MIB,
        48,
        [in_vmem(), anywhere()],
    )(rank, coupling, gain, solved, columns, *parts)


def plane_body(
    gain, schur, inverse, sens, residual, unit_rhs, start_state, active, unit_bus
):
    period = lax.axis_index("period")
    rank = lax.axis_index("bus").reshape(1)
    last = lax.axis_size("period") - 1
    everyone = tuple(range(last + 1))
    z, y = rank // 2, rank % 2
    far_end = (z == 0) | (z == 3)
    places = jnp.concatenate(
        [z, z ^ 1, jnp.where(far_end, z ^ 2, z ^ 3), jnp.where(far_end, z ^ 3, z ^ 2), y]
    )

    near, middle = bus_send(gain, 2, everyone), across(gain, everyone)
    *keep, send, solved = front(rank, active, unit_rhs, residual, inverse, sens)
    send, start_in = together(send, start_state)
    pieces = swap_z(start_pieces(rank, start_in), everyone)
    near, middle, send, keep, schur_in, pieces = together(
        near, middle, send, keep, schur, pieces
    )
    there = bus_send(send, 1, everyone)
    start = join(rank, pieces)
    middle2, third, there, columns = together(
        across(near, everyone),
        middle + outwards(middle, everyone),
        there,
        picked(rank, unit_bus, inverse),
    )
    fourth = middle2 + outwards(middle2, everyone)
    schur_y = bus_send(schur_cross(rank, schur_in), 1, everyone)
    terms = [mine + theirs.astype(F32) for mine, theirs in zip(keep, there, strict=True)]
    sent = [term.astype(BF16) for term in terms]
    start_y, fourth, from_end, from_middle, from_far = together(
        bus_send(start, 1, everyone),
        fourth,
        line_send(sent[1], ((0, 1), (3, 2)), everyone),
        across(jnp.stack([sent[3], sent[2]]), everyone),
        line_send(jnp.stack([sent[2], sent[3]]), ((0, 2), (3, 1)), everyone),
    )
    passed = outwards(
        (terms[1] + from_middle[1].astype(F32) + from_far[1].astype(F32)).astype(BF16), everyone
    )
    unit_right = (
        terms[0]
        + from_middle[0].astype(F32)
        + from_far[0].astype(F32)
        + from_end.astype(F32)
        + passed.astype(F32)
    )
    gain, near, third, fourth, unit_right, schur_y, columns, start, start_y = together(
        gain,
        near,
        third,
        fourth,
        unit_right,
        schur_y,
        columns,
        start,
        start_y,
    )

    sums, cross = unit_right.astype(BF16), jnp.zeros(unit_right.shape, BF16)
    for target in range(last - 1, -1, -1):
        vector = (
            period_send(sums, target + 1, target),
            cross if target == last - 1 else period_send(cross, target + 1, target, 1),
        )
        gain, near, third, fourth, sums, cross = together(gain, near, third, fourth, sums, cross)
        weights = [pack([gain, near, third]), fourth]
        sums, cross = backward(places, period == target, vector, unit_right, (sums, cross), weights)
    costate = (sums.astype(F32) + bus_send(cross, 1, everyone).astype(F32)).astype(BF16)
    product, cross, costate_rows = couple(
        rank, schur, schur_y, swap_z([costate] * 4, everyone)
    )
    *pieces, coupling = settle(rank, product, bus_send(cross, 1, everyone))
    driven = forward(places, (start, start_y), weights)
    advanced, coupled = finish(rank, driven, swap_z(pieces, everyone))

    state = (start, start_y)
    for target in range(1, last + 1):
        arrived = (
            period_send(advanced, target - 1, target),
            period_send(advanced, target - 1, target, 1),
        )
        state = tuple(
            jnp.where(period == target, new, old) for new, old in zip(arrived, state, strict=True)
        )
        if target < last:
            advanced = forward(places, arrived, weights, coupled)
    near = bus_send(jnp.stack(state), 2, everyone)
    own4, own6 = bus_send(state[0], 4, everyone), bus_send(state[0], 6, everyone)
    other4, other6 = bus_send(own4, 1, everyone), bus_send(own6, 1, everyone)
    storage, update = final(
        rank, coupling, gain, solved, columns, [*state, near, own4, other4, own6, other6]
    )
    return storage, costate_rows, update


def plain_body(
    gain, schur, inverse, sens, residual, unit_rhs, start_state, active, unit_bus
):
    period = lax.axis_index("period")
    rank = lax.axis_index("bus")
    size = lax.axis_size("bus")
    groups = lax.axis_size("period")
    units, whole = gain.shape
    buses, columns = residual.shape
    rows = columns // size

    def gathered(block):
        return lax.all_gather(block, "bus", axis=0, tiled=True)

    def to_columns(block):
        swapped = lax.all_to_all(block.reshape(size, rows, units), "bus", 0, 0)
        return jnp.transpose(swapped, (1, 0, 2)).reshape(rows, whole)

    weighted = residual * (1.0 + 3.0 * active.astype(F32))
    solve = times(inverse, weighted.astype(BF16)).astype(BF16)
    partial = lax.dot_general(solve, sens, (((0,), (0,)), ((), ())), preferred_element_type=F32)
    place = (0, rank * units)
    own = lax.dynamic_slice(partial, place, (columns, units)) + unit_rhs.T
    partial = lax.dynamic_update_slice(partial, own, place).astype(BF16)
    unit_right = lax.psum_scatter(partial, "bus", scatter_dimension=0, tiled=True).astype(F32)
    gain_whole = gathered(gain)
    costate = unit_right.astype(BF16)
    for target in range(groups - 2, -1, -1):
        later = period_send(costate, target + 1, target)
        current = (unit_right + times(later, gain_whole)).astype(BF16)
        costate = jnp.where(period == target, current, costate)
    costate_whole = gathered(costate)
    coupling = times_t(costate_whole, schur)
    coupled = to_columns(coupling.astype(BF16)).astype(F32)
    state = to_columns(start_state.T.astype(BF16))
    advanced = times_t(state, gain_whole) - coupled
    for target in range(1, groups):
        arrived = period_send(advanced.astype(BF16), target - 1, target)
        state = jnp.where(period == target, arrived, state)
        advanced = times_t(arrived, gain_whole) - coupled
    state_whole = gathered(state)
    storage = times_t(gain, state_whole) - coupling.T
    costate_rows = lax.dynamic_slice_in_dim(costate_whole, rank * units, units, 1).T.astype(F32)
    ids = rank * buses + jnp.arange(buses, dtype=jnp.int32)
    placement = (unit_bus == ids[:, None]).astype(BF16)
    network = (weighted - times_t(placement, state_whole)).astype(BF16)
    return storage, costate_rows, times(inverse, network)


def body(
    gain, schur, inverse_blocks, sensitivity, residual_bus, unit_rhs, start_state, active_set, unit_bus
):
    in_planes = lax.axis_size("bus") == 8 and lax.axis_size("period") > 2
    storage, costate, update = (plane_body if in_planes else plain_body)(
        gain[0],
        schur[0],
        inverse_blocks[0],
        sensitivity,
        residual_bus[0],
        unit_rhs[0],
        start_state,
        active_set[0][:, None],
        unit_bus[None, :],
    )
    return storage[None], costate[None], update[None]


def solution(mesh):
    by_period = P("period", "bus", None)
    placed = (
        by_period,
        by_period,
        by_period,
        P("bus", None),
        by_period,
        by_period,
        P("bus", None),
        P("period", "bus"),
        P(),
    )
    return jax.shard_map(
        body,
        mesh=mesh,
        in_specs=placed,
        out_specs=(by_period, by_period, by_period),
        check_vma=False,
    )
```

```python
import functools

import jax
import jax.numpy as jnp
from jax import lax
from jax.experimental import pallas as pl
from jax.experimental.pallas import tpu as pltpu
from jax.sharding import PartitionSpec as P

BOTH = ("period", "bus")
F32 = jnp.float32
BF16 = jnp.bfloat16
MIB = 1 << 20


def bus_send(block, flip, periods):
    size = lax.axis_size("bus")
    route = [(p * size + b, p * size + (b ^ flip)) for p in periods for b in range(size)]
    return lax.ppermute(block, BOTH, route)


def period_send(block, source, target, flip=0):
    size = lax.axis_size("bus")
    route = [(source * size + b, target * size + (b ^ flip)) for b in range(size)]
    return lax.ppermute(block, BOTH, route)


def times(left, right):
    return jnp.dot(left, right, preferred_element_type=F32)


def times_t(left, right):
    return lax.dot_general(left, right, (((1,), (1,)), ((), ())), preferred_element_type=F32)


def together(*values):
    return lax.optimization_barrier(values)


def line_send(block, pairs, periods):
    size = lax.axis_size("bus")
    route = [
        (p * size + 2 * source + y, p * size + 2 * target + y)
        for p in periods
        for source, target in pairs
        for y in range(2)
    ]
    return lax.ppermute(block, BOTH, route)


def across(block, periods):
    return line_send(block, ((1, 2), (2, 1)), periods)


def outwards(block, periods):
    return line_send(block, ((1, 0), (2, 3)), periods)


def swap_z(pieces, periods):
    return [pieces[0]] + [bus_send(pieces[flip // 2], flip, periods) for flip in (2, 4, 6)]


def in_vmem():
    return pl.BlockSpec(memory_space=pltpu.VMEM)


def anywhere():
    return pl.BlockSpec(memory_space=pl.ANY)


def in_smem():
    return pl.BlockSpec(memory_space=pltpu.SMEM)


def kernel_call(kernel, out_shape, in_specs, scratch, flops, bytes_accessed, mib, out_specs=None):
    return pl.pallas_call(
        kernel,
        out_shape=out_shape,
        in_specs=in_specs,
        out_specs=out_specs or jax.tree.map(lambda _: in_vmem(), out_shape),
        scratch_shapes=scratch,
        compiler_params=pltpu.CompilerParams(vmem_limit_bytes=mib * MIB),
        cost_estimate=pl.CostEstimate(
            flops=flops, bytes_accessed=bytes_accessed, transcendentals=0
        ),
    )


def at(index, size):
    return pl.ds(pl.multiple_of(index * size, size), size)


def front_kernel(
    rank_ref, active, rhs, residual_hbm, inverse_hbm, sens_hbm,
    k0, k2, k4, k6, send, solved,
    residual, inverse, sens, net, solve_t, partial, sems,
):
    rank = rank_ref[0]
    z, y = rank // 2, rank % 2
    loads = [
        pltpu.make_async_copy(residual_hbm, residual, sems.at[0]),
        pltpu.make_async_copy(inverse_hbm, inverse, sems.at[1]),
        pltpu.make_async_copy(sens_hbm, sens, sems.at[2]),
    ]
    for load in loads:
        load.start()
    loads[0].wait()
    net[...] = (residual[...] * (1.0 + 3.0 * active[...].astype(F32))).astype(BF16)
    loads[1].wait()
    blocks = inverse.shape[0] // 256

    @pl.loop(0, blocks)
    def _(i):
        rows = pl.ds(pl.multiple_of(i * 256, 256), 256)
        product = times(inverse[rows, :], net[...])
        solved[rows, :] = product
        solve_t[:, rows] = product.T.astype(BF16)

    loads[2].wait()

    @pl.loop(0, sens.shape[1] // 256)
    def _(i):
        columns = pl.ds(pl.multiple_of(i * 256, 256), 256)
        partial[:, columns] = times(solve_t[...], sens[:, columns])

    units = rhs.shape[0]
    partial[:, at(rank, units)] += rhs[...].T
    rows = k0.shape[0]
    for turn, out in enumerate((k0, k2, k4, k6)):
        here = at(z ^ turn, rows)
        for block in range(4):
            lanes = pl.ds(block * units, units)
            out[:, lanes] = partial[here, at(2 * block + y, units)]
            send[turn, :, lanes] = partial[here, at(2 * block + 1 - y, units)].astype(BF16)


def front(rank, active, rhs, residual, inverse, sens):
    buses, columns = residual.shape
    units = sens.shape[1]
    keep = jax.ShapeDtypeStruct((columns // 4, units // 2), F32)
    send = jax.ShapeDtypeStruct((4, columns // 4, units // 2), BF16)
    return kernel_call(
        front_kernel,
        [keep] * 4 + [send, jax.ShapeDtypeStruct((buses, columns), F32)],
        [in_smem(), in_vmem(), in_vmem(), anywhere(), anywhere(), anywhere()],
        [
            pltpu.VMEM((buses, columns), F32),
            pltpu.VMEM((buses, buses), BF16),
            pltpu.VMEM((buses, units), BF16),
            pltpu.VMEM((buses, columns), BF16),
            pltpu.VMEM((columns, buses), BF16),
            pltpu.VMEM((columns, units), F32),
            pltpu.SemaphoreType.DMA((3,)),
        ],
        2 * buses * columns * (buses + units),
        24 * MIB,
        48,
    )(rank, active, rhs, residual, inverse, sens)


def start_kernel(rank_ref, state, p0, p2, p4, p6):
    for turn, out in enumerate((p0, p2, p4, p6)):
        out[...] = state[:, at((rank_ref[0] // 2) ^ turn, out.shape[1])].astype(BF16)


def start_pieces(rank, state):
    units, columns = state.shape
    return kernel_call(
        start_kernel,
        [jax.ShapeDtypeStruct((units, columns // 4), BF16)] * 4,
        [in_smem(), in_vmem()],
        [],
        state.size,
        6 * state.size,
        8,
    )(rank, state)


def join_kernel(rank_ref, p0, p2, p4, p6, out):
    for turn, piece in enumerate((p0, p2, p4, p6)):
        out[at((rank_ref[0] // 2) ^ turn, piece.shape[0]), :] = piece[...]


def join(rank, pieces):
    units, rights = pieces[0].shape
    return kernel_call(
        join_kernel,
        jax.ShapeDtypeStruct((4 * units, rights), BF16),
        [in_smem()] + [in_vmem()] * 4,
        [],
        units * rights,
        16 * units * rights,
        8,
    )(rank, *pieces)


def pack_kernel(*refs):
    parts, (out, sems) = refs[:3], refs[3:]
    loads = [pltpu.make_async_copy(part, out.at[j], sems.at[j]) for j, part in enumerate(parts)]
    for load in loads:
        load.start()
    for load in loads:
        load.wait()


def pack(parts):
    return kernel_call(
        pack_kernel,
        jax.ShapeDtypeStruct((3, *parts[0].shape), BF16),
        [anywhere()] * 3,
        [pltpu.SemaphoreType.DMA((3,))],
        0,
        12 * parts[0].size,
        8,
    )(*parts)


def backward_kernel(places, turn, own, other, base, former_sums, former_cross, packed, fourth, sums, cross, total):
    units = fourth.shape[0]
    y = places[4]

    def step():
        vector = (own[...].astype(F32) + other[...].astype(F32)).astype(BF16)
        cross_like = jnp.zeros(total.shape, F32)
        total[...] = cross_like
        whole = packed.shape[2]
        for width in range(0, whole, 1024):
            lanes = pl.ds(width, 1024)
            product = None
            for place in range(4):
                weight = packed[place, :, lanes] if place < 3 else fourth[:, lanes]
                blocks = [
                    vector[:, z * units : (z + 1) * units] for z in range(4)
                ]
                chosen = blocks[0]
                for z in range(1, 4):
                    chosen = jnp.where(places[place] == z, blocks[z], chosen)
                term = times(chosen, weight)
                product = term if product is None else product + term
            total[:, lanes] = product
        for block in range(4):
            lanes = pl.ds(block * units, units)
            sums[:, lanes] = (base[:, lanes] + total[:, at(2 * block + y, units)]).astype(BF16)
            cross[:, lanes] = total[:, at(2 * block + 1 - y, units)].astype(BF16)

    def skip():
        sums[...] = former_sums[...]
        cross[...] = former_cross[...]

    pl.when(turn[0] == 1)(step)
    pl.when(turn[0] == 0)(skip)


def backward(places, turn, vector, base, former, weights):
    rows, half = base.shape
    out = jax.ShapeDtypeStruct((rows, half), BF16)
    return kernel_call(
        backward_kernel,
        [out, out],
        [in_smem()] * 2 + [in_vmem()] * 7,
        [pltpu.VMEM((rows, 2 * half), F32)],
        4 * rows * half * half,
        4 * half * half,
        12,
    )(places, turn.astype(jnp.int32).reshape(1), *vector, base, *former, *weights)


def forward_kernel(places, own, other, packed, fourth, *refs):
    subtracted, (out, state) = (refs[0], refs[1:]) if len(refs) > 2 else (None, refs)
    units = fourth.shape[0]
    y = places[4]
    for block in range(4):
        here = pl.ds(block * units, units)
        state[at(2 * block + y, units), :] = own[here, :]
        state[at(2 * block + 1 - y, units), :] = other[here, :]
    for place in range(4):
        weight = packed[place] if place < 3 else fourth[...]
        here = at(places[place], units)
        product = times(weight, state[...])
        if subtracted is not None:
            product = product - subtracted[here, :].astype(F32)
        out[here, :] = product.astype(out.dtype)


def forward(places, state, weights, subtracted=None):
    half, rights = state[0].shape
    extra = () if subtracted is None else (subtracted,)
    return kernel_call(
        forward_kernel,
        jax.ShapeDtypeStruct((half, rights), BF16 if extra else F32),
        [in_smem()] + [in_vmem()] * (4 + len(extra)),
        [pltpu.VMEM((2 * half, rights), BF16)],
        4 * rights * half * half,
        4 * half * half,
        12,
    )(places, *state, *weights, *extra)


def couple_kernel(rank_ref, schur, schur_y, c0, c2, c4, c6, product, cross, costate, whole, mine):
    z, y = rank_ref[0] // 2, rank_ref[0] % 2
    rows, units = c0.shape[0], schur.shape[0]
    for turn, part in enumerate((c0, c2, c4, c6)):
        whole[at(z ^ turn, rows), :] = part[...]
    for block in range(4):
        mine[:, pl.ds(block * units, units)] = schur[:, at(2 * block + y, units)]
    product[...] = times_t(whole[...], mine[...])
    cross[...] = times_t(whole[...], schur_y[...]).astype(BF16)
    costate[...] = whole[:, at(z, units)].astype(F32).T


def couple(rank, schur, schur_y, parts):
    units, half = schur_y.shape
    rows = parts[0].shape[0]
    return kernel_call(
        couple_kernel,
        [
            jax.ShapeDtypeStruct((4 * rows, units), F32),
            jax.ShapeDtypeStruct((4 * rows, units), BF16),
            jax.ShapeDtypeStruct((units, 4 * rows), F32),
        ],
        [in_smem()] + [in_vmem()] * 6,
        [pltpu.VMEM((4 * rows, half), BF16), pltpu.VMEM((units, half), BF16)],
        16 * rows * half * units,
        4 * MIB,
        16,
    )(rank, schur, schur_y, *parts)


def schur_kernel(rank_ref, schur, out):
    units = schur.shape[0]
    for block in range(4):
        out[:, pl.ds(block * units, units)] = schur[:, at(2 * block + 1 - rank_ref[0] % 2, units)]


def schur_cross(rank, schur):
    units, whole = schur.shape
    return kernel_call(
        schur_kernel,
        jax.ShapeDtypeStruct((units, whole // 2), BF16),
        [in_smem(), in_vmem()],
        [],
        units * whole,
        3 * units * whole,
        8,
    )(rank, schur)


def settle_kernel(rank_ref, product, cross, p0, p2, p4, p6, coupling):
    coupling[...] = (product[...] + cross[...].astype(F32)).T
    for turn, out in enumerate((p0, p2, p4, p6)):
        out[...] = coupling[:, at((rank_ref[0] // 2) ^ turn, out.shape[1])].astype(BF16)


def settle(rank, product, cross):
    columns, units = product.shape
    piece = jax.ShapeDtypeStruct((units, columns // 4), BF16)
    return kernel_call(
        settle_kernel,
        [piece] * 4 + [jax.ShapeDtypeStruct((units, columns), F32)],
        [in_smem()] + [in_vmem()] * 2,
        [],
        product.size,
        12 * product.size,
        8,
    )(rank, product, cross)


def finish_kernel(rank_ref, driven, p0, p2, p4, p6, out, terms):
    for turn, piece in enumerate((p0, p2, p4, p6)):
        here = at((rank_ref[0] // 2) ^ turn, piece.shape[0])
        out[here, :] = (driven[here, :] - piece[...].astype(F32)).astype(out.dtype)
        terms[here, :] = piece[...]


def finish(rank, driven, pieces):
    out = jax.ShapeDtypeStruct(driven.shape, BF16)
    return kernel_call(
        finish_kernel,
        [out, out],
        [in_smem()] + [in_vmem()] * 5,
        [],
        driven.size,
        10 * driven.size,
        8,
    )(rank, driven, *pieces)


def picked_kernel(rank_ref, unit_bus, inverse, out):
    buses = inverse.shape[0]
    ids = rank_ref[0] * buses + lax.broadcasted_iota(jnp.int32, (buses, 1), 0)

    @pl.loop(0, out.shape[1] // 256)
    def _(i):
        lanes = at(i, 256)
        placed = (unit_bus[:, lanes] == ids).astype(BF16)
        out[:, lanes] = times(inverse[...], placed).astype(BF16)


def picked(rank, unit_bus, inverse):
    buses, whole = inverse.shape[0], unit_bus.shape[1]
    return kernel_call(
        picked_kernel,
        jax.ShapeDtypeStruct((buses, whole), BF16),
        [in_smem(), in_vmem(), in_vmem()],
        [],
        2 * buses * buses * whole,
        12 * MIB,
        24,
    )(rank, unit_bus, inverse)


def final_kernel(
    rank_ref, coupling, gain, solved_hbm, columns_hbm,
    own, other, near, own4, other4, own6, other6,
    storage, update, solved, columns, whole, sems,
):
    rank = rank_ref[0]
    z, y = rank // 2, rank % 2
    blocks = columns.shape[0] // 256
    sources = ((columns_hbm, columns), (solved_hbm, solved))

    def transfer(i, kind):
        here = at(i, 256)
        if kind == 2:
            return pltpu.make_async_copy(solved.at[here], update.at[here], sems.at[2, i])
        source, target = sources[kind]
        return pltpu.make_async_copy(source.at[here], target.at[here], sems.at[kind, i])

    @pl.loop(0, blocks)
    def _(i):
        for kind in range(2):
            transfer(i, kind).start()

    rights, units = own.shape[1], gain.shape[0]

    def put(turn, halves):
        for block in range(4):
            lanes = slice(block * units, (block + 1) * units)
            for place, half in enumerate(halves):
                which = y if place == 0 else 1 - y
                whole[at(2 * block + which, units), at(z ^ turn, rights)] = half[lanes, :]

    put(0, (own[...], other[...]))
    put(1, (near[0], near[1]))
    put(2, (own4[...], other4[...]))
    put(3, (own6[...], other6[...]))
    storage[...] = times(gain[...], whole[...]) - coupling[...]

    @pl.loop(0, blocks)
    def _(i):
        here = at(i, 256)
        for kind in range(2):
            transfer(i, kind).wait()
        solved[here, :] = solved[here, :] - times(columns[here, :], whole[...])
        transfer(i, 2).start()

    @pl.loop(0, blocks)
    def _(i):
        transfer(i, 2).wait()


def final(rank, coupling, gain, solved, columns, parts):
    buses, rights = solved.shape
    units, whole = gain.shape
    return kernel_call(
        final_kernel,
        [
            jax.ShapeDtypeStruct((units, rights), F32),
            jax.ShapeDtypeStruct((buses, rights), F32),
        ],
        [in_smem()] + [in_vmem()] * 2 + [anywhere()] * 2 + [in_vmem()] * 7,
        [
            pltpu.VMEM((buses, rights), F32),
            pltpu.VMEM((buses, whole), BF16),
            pltpu.VMEM((whole, rights), BF16),
            pltpu.SemaphoreType.DMA((3, buses // 256)),
        ],
        2 * rights * (buses + units) * whole,
        24 * MIB,
        48,
        [in_vmem(), anywhere()],
    )(rank, coupling, gain, solved, columns, *parts)


def plane_body(
    gain, schur, inverse, sens, residual, unit_rhs, start_state, active, unit_bus
):
    period = lax.axis_index("period")
    rank = lax.axis_index("bus").reshape(1)
    last = lax.axis_size("period") - 1
    everyone = tuple(range(last + 1))
    z, y = rank // 2, rank % 2
    far_end = (z == 0) | (z == 3)
    places = jnp.concatenate(
        [z, z ^ 1, jnp.where(far_end, z ^ 2, z ^ 3), jnp.where(far_end, z ^ 3, z ^ 2), y]
    )

    near, middle = bus_send(gain, 2, everyone), across(gain, everyone)
    *keep, send, solved = front(rank, active, unit_rhs, residual, inverse, sens)
    send, start_in = together(send, start_state)
    pieces = swap_z(start_pieces(rank, start_in), (0,))
    near, middle, send, keep, schur_in, pieces = together(
        near, middle, send, keep, schur, pieces
    )
    there = bus_send(send, 1, everyone)
    start = join(rank, pieces)
    middle2, third, there, columns = together(
        across(near, everyone),
        middle + outwards(middle, everyone),
        there,
        picked(rank, unit_bus, inverse),
    )
    fourth = middle2 + outwards(middle2, everyone)
    schur_y = bus_send(schur_cross(rank, schur_in), 1, everyone)
    terms = [mine + theirs.astype(F32) for mine, theirs in zip(keep, there, strict=True)]
    sent = [term.astype(BF16) for term in terms]
    start_y, fourth, from_end, from_middle, from_far = together(
        bus_send(start, 1, (0,)),
        fourth,
        line_send(sent[1], ((0, 1), (3, 2)), everyone),
        across(jnp.stack([sent[3], sent[2]]), everyone),
        line_send(jnp.stack([sent[2], sent[3]]), ((0, 2), (3, 1)), everyone),
    )
    passed = outwards(
        (terms[1] + from_middle[1].astype(F32) + from_far[1].astype(F32)).astype(BF16), everyone
    )
    unit_right = (
        terms[0]
        + from_middle[0].astype(F32)
        + from_far[0].astype(F32)
        + from_end.astype(F32)
        + passed.astype(F32)
    )
    gain, near, third, fourth, unit_right, schur_y, columns, start, start_y = together(
        gain,
        near,
        third,
        fourth,
        unit_right,
        schur_y,
        columns,
        start,
        start_y,
    )

    sums, cross = unit_right.astype(BF16), jnp.zeros(unit_right.shape, BF16)
    for target in range(last - 1, -1, -1):
        vector = (
            period_send(sums, target + 1, target),
            cross if target == last - 1 else period_send(cross, target + 1, target, 1),
        )
        gain, near, third, fourth, sums, cross = together(gain, near, third, fourth, sums, cross)
        weights = [pack([gain, near, third]), fourth]
        sums, cross = backward(places, period == target, vector, unit_right, (sums, cross), weights)
    costate = (sums.astype(F32) + bus_send(cross, 1, everyone).astype(F32)).astype(BF16)
    product, cross, costate_rows = couple(
        rank, schur, schur_y, swap_z([costate] * 4, everyone)
    )
    *pieces, coupling = settle(rank, product, bus_send(cross, 1, everyone))
    driven = forward(places, (start, start_y), weights)
    advanced, coupled = finish(rank, driven, swap_z(pieces, everyone))

    state = (start, start_y)
    for target in range(1, last + 1):
        arrived = (
            period_send(advanced, target - 1, target),
            period_send(advanced, target - 1, target, 1),
        )
        state = tuple(
            jnp.where(period == target, new, old) for new, old in zip(arrived, state, strict=True)
        )
        if target < last:
            advanced = forward(places, arrived, weights, coupled)
    near = bus_send(jnp.stack(state), 2, everyone)
    own4, own6 = bus_send(state[0], 4, everyone), bus_send(state[0], 6, everyone)
    other4, other6 = bus_send(own4, 1, everyone), bus_send(own6, 1, everyone)
    storage, update = final(
        rank, coupling, gain, solved, columns, [*state, near, own4, other4, own6, other6]
    )
    return storage, costate_rows, update


def plain_body(
    gain, schur, inverse, sens, residual, unit_rhs, start_state, active, unit_bus
):
    period = lax.axis_index("period")
    rank = lax.axis_index("bus")
    size = lax.axis_size("bus")
    groups = lax.axis_size("period")
    units, whole = gain.shape
    buses, columns = residual.shape
    rows = columns // size

    def gathered(block):
        return lax.all_gather(block, "bus", axis=0, tiled=True)

    def to_columns(block):
        swapped = lax.all_to_all(block.reshape(size, rows, units), "bus", 0, 0)
        return jnp.transpose(swapped, (1, 0, 2)).reshape(rows, whole)

    weighted = residual * (1.0 + 3.0 * active.astype(F32))
    solve = times(inverse, weighted.astype(BF16)).astype(BF16)
    partial = lax.dot_general(solve, sens, (((0,), (0,)), ((), ())), preferred_element_type=F32)
    place = (0, rank * units)
    own = lax.dynamic_slice(partial, place, (columns, units)) + unit_rhs.T
    partial = lax.dynamic_update_slice(partial, own, place).astype(BF16)
    unit_right = lax.psum_scatter(partial, "bus", scatter_dimension=0, tiled=True).astype(F32)
    gain_whole = gathered(gain)
    costate = unit_right.astype(BF16)
    for target in range(groups - 2, -1, -1):
        later = period_send(costate, target + 1, target)
        current = (unit_right + times(later, gain_whole)).astype(BF16)
        costate = jnp.where(period == target, current, costate)
    costate_whole = gathered(costate)
    coupling = times_t(costate_whole, schur)
    coupled = to_columns(coupling.astype(BF16)).astype(F32)
    state = to_columns(start_state.T.astype(BF16))
    advanced = times_t(state, gain_whole) - coupled
    for target in range(1, groups):
        arrived = period_send(advanced.astype(BF16), target - 1, target)
        state = jnp.where(period == target, arrived, state)
        advanced = times_t(arrived, gain_whole) - coupled
    state_whole = gathered(state)
    storage = times_t(gain, state_whole) - coupling.T
    costate_rows = lax.dynamic_slice_in_dim(costate_whole, rank * units, units, 1).T.astype(F32)
    ids = rank * buses + jnp.arange(buses, dtype=jnp.int32)
    placement = (unit_bus == ids[:, None]).astype(BF16)
    network = (weighted - times_t(placement, state_whole)).astype(BF16)
    return storage, costate_rows, times(inverse, network)


def body(
    gain, schur, inverse_blocks, sensitivity, residual_bus, unit_rhs, start_state, active_set, unit_bus
):
    in_planes = lax.axis_size("bus") == 8 and lax.axis_size("period") > 2
    storage, costate, update = (plane_body if in_planes else plain_body)(
        gain[0],
        schur[0],
        inverse_blocks[0],
        sensitivity,
        residual_bus[0],
        unit_rhs[0],
        start_state,
        active_set[0][:, None],
        unit_bus[None, :],
    )
    return storage[None], costate[None], update[None]


def solution(mesh):
    by_period = P("period", "bus", None)
    placed = (
        by_period,
        by_period,
        by_period,
        P("bus", None),
        by_period,
        by_period,
        P("bus", None),
        P("period", "bus"),
        P(),
    )
    return jax.shard_map(
        body,
        mesh=mesh,
        in_specs=placed,
        out_specs=(by_period, by_period, by_period),
        check_vma=False,
    )
```
